256 devices in a mesh: band: 8 (over y, core), member: 32 (over x, z).
Axes of the slice: x: 4, y: 4, z: 8, core: 2. Of those that a mesh axis runs over, the one named last changes fastest.
Arguments:
- ensemble: bfloat16 [256, 4, 256, 1024], P('member', None, 'band'), may hold values from -6 to 6
- variance: float32 [4, 256, 1024], P(None, 'band'), may hold values from 0.25 to 4
- obs_index: int32 [32, 32768], P('member', 'band'), may hold values from 0 to 131071
- obs_value: float32 [32, 32768], P('member', 'band'), may hold values from -8 to 8
- obs_error: float32 [32, 32768], P('member', 'band'), may hold values from 0.5 to 2
- root_ranks: int32 [2], replicated, may hold values from 0 to 31
Outputs:
- increment: float32 [4, 256, 1024], P(None, 'band')
The draws below stay inside these ranges and needn't reach their ends.
Inputs may be any that keep to these rules, and one draw needn't show every extreme that they name: `obs_index`: the position level * 32 * 1024 + row within the band * 1024 + longitude; columns b * 4096 to (b + 1) * 4096 - 1 belong to band b; positions may repeat.
All inputs are finite; a program needn't handle non-finite values.
Results may differ from the reference program's by a relative error of at most 0.0024.
Values may be sent and summed in bfloat16 or wider, within the bound.
A program may use at most 64 MiB of HBM per device.

```python
import math
import jax
import jax.numpy as jnp
from jax import lax

LEV = 4
LAT_DEV = 32
LON = 1024
HALF = 8
MEM_DEV = 8
NOBS = 4096
ITERS = 2
MEMBERS = 256
NLAT = 256
BLOCKS = 32
BANDOBS = 32768
N_BAND = 8
N_MEMBER = 32


def place_ends(entries, stream_key, least, largest):
    extent = entries.shape
    spot = [jax.random.randint(jax.random.fold_in(stream_key, axis), (), 0, extent[axis]) for axis in range(len(extent))]
    entries = entries.at[tuple(spot)].set(least)
    longest = extent.index(max(extent))
    spot[longest] = (spot[longest] + 1) % extent[longest]
    return entries.at[tuple(spot)].set(largest)


def steps_of(rng, dims, shards, smallest, high):
    factor_of, own = 1.0, jax.random.fold_in(rng, 6)
    for position, shards_of in shards:
        draws = jnp.exp(jax.random.uniform(jax.random.fold_in(own, position), (shards_of,), jnp.float32, smallest / len(shards), high / len(shards)))
        factor_of = factor_of * jnp.repeat(draws, dims[position] // shards_of).reshape([-1 if axis == position else 1 for axis in range(len(dims))])
    return factor_of


def scatter_about(rng, extent, width, reach, cuts=(), kind=jnp.bfloat16):
    factor_of = steps_of(rng, extent, cuts, -0.22, 0.18) if cuts else 1.0
    array = jax.random.normal(rng, extent, jnp.float32) * width * factor_of
    return jnp.minimum(jnp.maximum(array, -reach), reach).astype(kind)


def setup_inputs(seed: int = 0) -> dict:
    streams_of = jax.random.split(jax.random.key(seed), 7)
    ensemble = scatter_about(streams_of[0], (MEMBERS, LEV, NLAT, LON), 1.0, 6.0, ((0, 32), (2, 8)))
    variance = jnp.clip(jnp.exp(math.log(4.0) - 2.7725887 * jax.random.uniform(streams_of[1], (LEV, NLAT, LON), jnp.float32) ** steps_of(streams_of[1], (LEV, NLAT, LON), ((1, 8),), -0.2, 0.2)), 0.25, 4.0)
    obs_index = place_ends(jax.random.randint(streams_of[2], (BLOCKS, BANDOBS), 0, LEV * LAT_DEV * LON), jax.random.fold_in(streams_of[2], 1), 0, (LEV * LAT_DEV * LON) - 1).astype(jnp.int32)
    obs_value = scatter_about(streams_of[3], (BLOCKS, BANDOBS), 2.0, 8.0, ((0, 32), (1, 8)), jnp.float32)
    obs_error = jnp.clip(jnp.exp(math.log(2.0) - 1.3862944 * jax.random.uniform(streams_of[4], (BLOCKS, BANDOBS), jnp.float32) ** steps_of(streams_of[4], (BLOCKS, BANDOBS), ((0, 32), (1, 8)), -0.2, 0.2)), 0.5, 2.0)
    root_ranks = jax.random.randint(streams_of[5], (ITERS,), 0, N_MEMBER).astype(jnp.int32)
    return dict(ensemble=ensemble, variance=variance, obs_index=obs_index, obs_value=obs_value, obs_error=obs_error, root_ranks=root_ranks)


huber_edge = 1.5
ensemble_share = 0.75
static_share = 0.25

def tap_table(radius):
    offsets = jnp.arange(-radius, radius + 1).astype(jnp.float32)
    raw = jnp.exp(-0.5 * (offsets / (0.5 * radius)) ** 2)
    return (raw / jnp.sqrt(jnp.sum(raw * raw))).astype(jnp.bfloat16).astype(jnp.float32)

def along_lon(values, table):
    source = values.astype(jnp.float32)
    total = jnp.zeros(source.shape, jnp.float32)
    for shift in range(-HALF, HALF + 1):
        total = total + table[shift + HALF] * jnp.roll(source, shift, axis=-1)
    return total

def along_lat(values, table):
    source = values.astype(jnp.float32)
    padded = jnp.pad(source, ((0, 0), (0, 0), (HALF, HALF), (0, 0)))
    total = jnp.zeros(source.shape, jnp.float32)
    for shift in range(-HALF, HALF + 1):
        total = total + table[shift + HALF] * padded[:, :, HALF + shift:HALF + shift + NLAT, :]
    return total

def reference(ensemble, variance, obs_index, obs_value, obs_error, root_ranks):
    table = tap_table(HALF)
    field = jnp.zeros((LEV, NLAT, LON), jnp.float32)
    band_of = (jnp.arange(NOBS * N_BAND) // NOBS).astype(jnp.int32)
    blocks = ensemble.reshape(N_MEMBER, MEM_DEV, LEV, NLAT, LON)
    for iteration in range(ITERS):
        block = root_ranks[iteration]
        local = obs_index[block].astype(jnp.int32)
        level = local // (LAT_DEV * LON)
        row_pos = band_of * LAT_DEV + local // LON % LAT_DEV
        column = local % LON
        place = ((level * NLAT + row_pos) * LON + column).astype(jnp.int32)
        values = obs_value[block]
        errors = obs_error[block]
        departure = values - field.reshape(-1)[place]
        weight = huber_edge / jnp.maximum(jnp.abs(departure / errors), huber_edge)
        gradient = jnp.zeros((LEV * NLAT * LON,), jnp.float32).at[place].add(weight * departure / (errors * errors)).reshape(LEV, NLAT, LON)

        def one_block(total, members):
            wide = members.astype(jnp.float32)
            mixed = (wide * gradient[None]).astype(jnp.bfloat16)
            first = along_lon(mixed, table).astype(jnp.bfloat16)
            first = along_lat(first, table).astype(jnp.bfloat16)
            second = along_lon(first, table).astype(jnp.bfloat16)
            second = along_lat(second, table)
            return (total + lax.optimization_barrier(jnp.sum(wide * second, axis=0)), None)
        spread, _ = lax.scan(one_block, jnp.zeros((LEV, NLAT, LON), jnp.float32), blocks)
        direction = ensemble_share * spread / (MEMBERS - 1) + static_share * variance * gradient
        along = jnp.sum(gradient * direction)
        back = jnp.sum(field * gradient)
        reached = direction.reshape(-1)[place]
        curve = jnp.sum(weight * reached * reached / (errors * errors))
        field = field + (along - back) / (along + curve) * direction
    return field
```

```python
import functools
import math

import jax
import jax.numpy as jnp
from jax import lax
from jax.experimental import pallas as pl
from jax.experimental.pallas import tpu as pltpu
from jax.sharding import PartitionSpec as P

HALF = 8
ITERS = 2
LANE = 128
HALO = 2 * HALF
BLK = 256
QUAD = 4
GROUP = 4

huber_edge = 1.5
ensemble_share = 0.75
static_share = 0.25

F32 = jnp.float32
BF16 = jnp.bfloat16


def taps(distance, keep):
    raw = [math.exp(-0.5 * (k / (0.5 * HALF)) ** 2) for k in range(-HALF, HALF + 1)]
    norm = math.sqrt(sum(r * r for r in raw))
    scaled = distance.astype(F32) / (0.5 * HALF)
    entry = jnp.exp(-0.5 * scaled * scaled) / norm
    keep = keep & (jnp.abs(distance) <= HALF)
    return jnp.where(keep, entry, 0.0).astype(BF16)


def iota(shape, dim):
    return lax.broadcasted_iota(jnp.int32, shape, dim)


def split(x):
    hi = x.astype(BF16).astype(F32)
    return hi, x - hi


def kernel(
    n_band, n_member, members_here, levels, lat, lon,
    root_ref, ens_ref, var_ref, idx_ref, val_ref, err_ref, out_ref,
    ext, wlon, lat1, lat2, send_obs, got_obs, obs, hot, grad, grad2, gpad,
    xpad, ypad, zpad, vpad, spread, arrived, varp, direc, split_dir,
    sums, band_sums, total_sums, member_sums,
    own_sem, ens_send, ens_recv, obs_send, obs_recv, halo_send, halo_recv,
    rs_send, rs_recv, ag_send, ag_recv, sc_send, sc_recv,
):
    me = lax.axis_index("member")
    band = lax.axis_index("band")
    rest = n_member - 1
    cols = lon // LANE
    wide = lat + 2 * HALO
    mid = lat + 2 * HALF
    rows = levels * lat
    up = lax.rem(band + 1, n_band)
    down = lax.rem(band + n_band - 1, n_band)
    my_row = pl.multiple_of((me // cols) * 8, 8)
    my_col = pl.multiple_of((me % cols) * LANE, LANE)

    def remote(src, dst, send, recv, to_band, to_member):
        return pltpu.make_async_remote_copy(
            src_ref=src, dst_ref=dst, send_sem=send, recv_sem=recv,
            device_id=(to_band, to_member), device_id_type=pl.DeviceIdType.MESH,
        )

    def drain(ref, sem):
        pltpu.make_async_copy(ref, ref, sem).wait()

    def to_members(start):
        def body(k, carry):
            start(k, lax.rem(me + k, n_member))
            return carry
        lax.fori_loop(1, n_member, body, 0)

    barrier = pltpu.get_barrier_semaphore()

    def greet_member(k, peer):
        pl.semaphore_signal(barrier, inc=1, device_id=(band, peer), device_id_type=pl.DeviceIdType.MESH)

    to_members(greet_member)

    def greet_band(k, carry):
        pl.semaphore_signal(
            barrier, inc=1, device_id=(lax.rem(band + k, n_band), me), device_id_type=pl.DeviceIdType.MESH
        )
        return carry

    lax.fori_loop(1, n_band, greet_band, 0)

    own = pltpu.make_async_copy(ens_ref, ext.at[:, :, pl.ds(HALO, lat), :], own_sem.at[0])
    own.start()
    own_var = pltpu.make_async_copy(
        var_ref.at[:, pl.ds(my_row, 8), pl.ds(my_col, LANE)], varp, own_sem.at[1]
    )
    own_var.start()

    flags = [(root_ref[it] == me).astype(F32) for it in range(ITERS)]
    for j in range(n_member):
        at = pl.ds(j * LANE, LANE)
        parts = [idx_ref[0:1, at].astype(F32), val_ref[0:1, at], err_ref[0:1, at]]
        lines = [part * flags[it] for it in range(ITERS) for part in parts]
        send_obs[j] = jnp.concatenate(lines + [jnp.zeros((2, LANE), F32)], axis=0)

    pl.semaphore_wait(barrier, n_member - 1 + n_band - 1)

    to_members(
        lambda k, peer: remote(
            send_obs.at[peer], got_obs.at[k - 1], obs_send.at[0], obs_recv.at[0], band, peer
        ).start()
    )
    ens_up = remote(
        ens_ref.at[:, :, pl.ds(lat - HALO, HALO), :], ext.at[:, :, pl.ds(0, HALO), :],
        ens_send.at[0], ens_recv.at[0], up, me,
    )
    ens_down = remote(
        ens_ref.at[:, :, pl.ds(0, HALO), :], ext.at[:, :, pl.ds(HALO + lat, HALO), :],
        ens_send.at[1], ens_recv.at[1], down, me,
    )
    ens_up.start()
    ens_down.start()

    shape = (2 * BLK, BLK)
    wlon[...] = taps(iota(shape, 1) - iota(shape, 0) + LANE, iota(shape, 0) >= 0)
    shape = (QUAD * mid, QUAD * wide)
    target, source = iota(shape, 0), iota(shape, 1)
    row_out = band * lat - HALF + target % mid
    row_in = band * lat - HALO + source % wide
    all_rows = n_band * lat
    lat1[...] = taps(
        row_in - row_out,
        (target // mid == source // wide)
        & (row_out >= 0) & (row_out < all_rows) & (row_in >= 0) & (row_in < all_rows),
    )
    shape = (QUAD * lat, QUAD * mid)
    target, source = iota(shape, 0), iota(shape, 1)
    lat2[...] = taps(source % mid - HALF - target % lat, target // lat == source // mid)

    drain(got_obs, obs_recv.at[0])
    obs[me] = send_obs[me] + jnp.sum(got_obs[...], axis=0)
    to_members(
        lambda k, peer: remote(
            obs.at[me], obs.at[me], obs_send.at[1], obs_recv.at[1], band, peer
        ).start()
    )
    drain(got_obs, obs_recv.at[1])

    groups = n_member // GROUP
    width = GROUP * LANE

    def line(g, which):
        return jnp.concatenate([obs[g * GROUP + j, which : which + 1, :] for j in range(GROUP)], axis=1)

    def build_hot(it):
        def body(g, carry):
            column = line(g, 3 * it).astype(jnp.int32) % lon
            for r in range(0, lon, LANE):
                hit = iota((LANE, width), 0) + r == column
                hot[g, r : r + LANE, :] = jnp.where(hit, 1.0, 0.0).astype(BF16)
            return carry
        lax.fori_loop(0, groups, body, 0)

    nt = (((1,), (1,)), ((), ()))

    def build_gradient(it, step):
        grad[...] = jnp.zeros_like(grad)
        grad2[...] = jnp.zeros_like(grad2)

        def body(g, carry):
            place = line(g, 3 * it).astype(jnp.int32)
            values = line(g, 3 * it + 1)
            errors = line(g, 3 * it + 2)
            row = place // lon
            departure = values
            if it > 0:
                level, in_level = row // lat, row % lat
                line_of = (in_level // 8) * (8 * levels) + level * 8 + in_level % 8
                found = jnp.dot(split_dir[...], hot[g], preferred_element_type=F32)
                found = found[:rows] + found[rows:]
                reached = jnp.sum(jnp.where(iota((rows, width), 0) == line_of, found, 0.0), axis=0, keepdims=True)
                departure = values - step * reached
            weight = huber_edge / jnp.maximum(jnp.abs(departure / errors), huber_edge)
            square = errors * errors
            hit = iota((rows, width), 0) == row
            terms = [jnp.where(hit, part, 0.0).astype(BF16) for part in split(weight * departure / square)]
            grad[...] += lax.dot_general(jnp.concatenate(terms, axis=0), hot[g], nt, preferred_element_type=F32)
            mine = iota((8 * levels, width), 0)
            hit = (mine // 8) * lat + my_row + mine % 8 == row
            terms = [jnp.where(hit, part, 0.0).astype(BF16) for part in split(weight / square)]
            grad2[...] += lax.dot_general(
                jnp.concatenate(terms, axis=0), hot[g, pl.ds(my_col, LANE), :], nt, preferred_element_type=F32
            )
            return carry

        lax.fori_loop(0, groups, body, 0)
        for level in range(levels):
            a, b = level * lat, rows + level * lat
            gpad[it, level, HALO : HALO + lat, :] = grad[a : a + lat, :] + grad[b : b + lat, :]

    def lon_filter(padded, store):
        for c in range(0, lon, BLK):
            at = slice(c, c + BLK)
            store(at, jnp.dot(padded[:, c : c + 2 * BLK], wlon[...], preferred_element_type=F32).astype(BF16))

    def put_padded(ref, at, block):
        ref[:, LANE + at.start : LANE + at.stop] = block
        if at.start == 0:
            ref[:, LANE + lon :] = block[:, :LANE]
        if at.stop == lon:
            ref[:, :LANE] = block[:, block.shape[1] - LANE :]

    def filters(it, level):
        for h in range(members_here // QUAD):
            who = slice(h * QUAD, (h + 1) * QUAD)
            xs, ys, zs, vs = xpad.at[h], ypad.at[h], zpad.at[h], vpad.at[h]
            for c in range(0, lon, BLK):
                at = slice(c, c + BLK)
                mixed = ext[who, level, :, at].astype(F32) * gpad[it, level, :, at][None]
                put_padded(xs, at, mixed.astype(BF16).reshape(QUAD * wide, BLK))

            def store_y(at, block):
                ys[:, at] = block

            lon_filter(xs, store_y)
            for c in range(0, lon, BLK):
                at = slice(c, c + BLK)
                put_padded(zs, at, jnp.dot(lat1[...], ys[:, at], preferred_element_type=F32).astype(BF16))

            def store_v(at, block):
                vs[:, at] = block

            lon_filter(zs, store_v)
            for c in range(0, lon, BLK):
                at = slice(c, c + BLK)
                second = jnp.dot(lat2[...], vs[:, at], preferred_element_type=F32).reshape(QUAD, lat, BLK)
                part = jnp.sum(ext[who, level, HALO : HALO + lat, at].astype(F32) * second, axis=0)
                if h == 0:
                    spread[it, level, :, at] = part
                else:
                    spread[it, level, :, at] += part

    steps = []
    fields = []
    build_hot(0)
    for it in range(ITERS):
        build_gradient(it, steps[-1] if steps else None)
        halo_up = remote(
            gpad.at[it, :, pl.ds(lat, HALO), :], gpad.at[it, :, pl.ds(0, HALO), :],
            halo_send.at[it, 0], halo_recv.at[it, 0], up, me,
        )
        halo_down = remote(
            gpad.at[it, :, pl.ds(HALO, HALO), :], gpad.at[it, :, pl.ds(HALO + lat, HALO), :],
            halo_send.at[it, 1], halo_recv.at[it, 1], down, me,
        )
        halo_up.start()
        halo_down.start()
        if it == 0:
            own.wait()
            own_var.wait()
            ens_up.wait()
            ens_down.wait()
        halo_up.wait()
        halo_down.wait()

        def level_body(level, carry):
            filters(it, level)

            def send(k, peer):
                row = pl.multiple_of((peer // cols) * 8, 8)
                col = pl.multiple_of((peer % cols) * LANE, LANE)
                remote(
                    spread.at[it, level, pl.ds(row, 8), pl.ds(col, LANE)], arrived.at[it, level, k - 1],
                    rs_send.at[it, level], rs_recv.at[it, level], band, peer,
                ).start()

            to_members(send)
            return carry

        lax.fori_loop(0, levels, level_body, 0)

        along = jnp.zeros((8, LANE), F32)
        back = jnp.zeros((8, LANE), F32)
        curve = jnp.zeros((8, LANE), F32)
        pieces = []
        for level in range(levels):
            drain(arrived.at[it, level], rs_recv.at[it, level])
            summed = spread[it, level, pl.ds(my_row, 8), pl.ds(my_col, LANE)] + jnp.sum(arrived[it, level], axis=0)
            g = gpad[it, level, pl.ds(HALO + my_row, 8), pl.ds(my_col, LANE)]
            d = ensemble_share * summed / (members_here * n_member - 1) + static_share * varp[level] * g
            a = level * 8
            c = grad2[a : a + 8, :] + grad2[a + 8 * levels : a + 8 * levels + 8, :]
            along += g * d
            curve += c * d * d
            if it > 0:
                back += fields[-1][level] * g
            direc[it, me // cols, a : a + 8, pl.ds(my_col, LANE)] = d
            pieces.append(d)
        sums[it] = jnp.concatenate(
            [jnp.sum(x, axis=0, keepdims=True) for x in (along, back, curve)] + [jnp.zeros((5, LANE), F32)], axis=0
        )

        def send_sums(k, carry):
            remote(
                sums.at[it], band_sums.at[it, k - 1], sc_send.at[it, 0], sc_recv.at[it, 0],
                lax.rem(band + k, n_band), me,
            ).start()
            return carry

        lax.fori_loop(1, n_band, send_sums, 0)

        def send_piece(k, peer):
            piece = direc.at[it, me // cols, :, pl.ds(my_col, LANE)]
            remote(piece, piece, ag_send.at[it], ag_recv.at[it], band, peer).start()

        to_members(send_piece)
        if it + 1 < ITERS:
            build_hot(it + 1)
        drain(band_sums.at[it], sc_recv.at[it, 0])
        total_sums[it] = sums[it] + jnp.sum(band_sums[it], axis=0)
        to_members(
            lambda k, peer: remote(
                total_sums.at[it], member_sums.at[it, k - 1], sc_send.at[it, 1], sc_recv.at[it, 1], band, peer
            ).start()
        )
        drain(member_sums.at[it], sc_recv.at[it, 1])
        total = jnp.sum(total_sums[it] + jnp.sum(member_sums[it], axis=0), axis=1, keepdims=True)
        step = (total[0:1] - total[1:2]) / (total[0:1] + total[2:3])
        steps.append(step)
        fields.append([step * d for d in pieces])
        drain(arrived.at[it], ag_recv.at[it])
        if it + 1 < ITERS:
            for r in range(lat // 8):
                a = r * 8 * levels
                hi, lo = split(direc[it, r])
                split_dir[a : a + 8 * levels, :] = hi.astype(BF16)
                split_dir[rows + a : rows + a + 8 * levels, :] = lo.astype(BF16)

    for level in range(levels):
        for r in range(lat // 8):
            a = level * 8
            out_ref[level, r * 8 : r * 8 + 8, :] = (
                steps[0] * direc[0, r, a : a + 8, :] + steps[1] * direc[1, r, a : a + 8, :]
            )

    drain(got_obs, obs_send.at[0])
    drain(got_obs, obs_send.at[1])
    for it in range(ITERS):
        for level in range(levels):
            drain(arrived.at[it, level], rs_send.at[it, level])
        drain(arrived.at[it], ag_send.at[it])
        drain(band_sums.at[it], sc_send.at[it, 0])
        drain(member_sums.at[it], sc_send.at[it, 1])


def local(n_band, n_member, ensemble, variance, obs_index, obs_value, obs_error, root_ranks):
    members_here, levels, lat, lon = ensemble.shape
    wide, mid, rows = lat + 2 * HALO, lat + 2 * HALF, levels * lat
    halves = members_here // QUAD
    rest = n_member - 1
    dma = pltpu.SemaphoreType.DMA
    vmem = pl.BlockSpec(memory_space=pltpu.VMEM)
    hbm = pl.BlockSpec(memory_space=pl.ANY)
    return pl.pallas_call(
        functools.partial(kernel, n_band, n_member, members_here, levels, lat, lon),
        out_shape=jax.ShapeDtypeStruct((levels, lat, lon), F32),
        in_specs=[pl.BlockSpec(memory_space=pltpu.SMEM), hbm, hbm, vmem, vmem, vmem],
        out_specs=vmem,
        scratch_shapes=[
            pltpu.VMEM((members_here, levels, wide, lon), BF16),
            pltpu.VMEM((2 * BLK, BLK), BF16),
            pltpu.VMEM((QUAD * mid, QUAD * wide), BF16),
            pltpu.VMEM((QUAD * lat, QUAD * mid), BF16),
            pltpu.VMEM((n_member, 8, LANE), F32),
            pltpu.VMEM((rest, 8, LANE), F32),
            pltpu.VMEM((n_member, 8, LANE), F32),
            pltpu.VMEM((n_member // GROUP, lon, GROUP * LANE), BF16),
            pltpu.VMEM((2 * rows, lon), F32),
            pltpu.VMEM((2 * 8 * levels, LANE), F32),
            pltpu.VMEM((ITERS, levels, wide, lon), F32),
            pltpu.VMEM((halves, QUAD * wide, lon + 2 * LANE), BF16),
            pltpu.VMEM((halves, QUAD * wide, lon), BF16),
            pltpu.VMEM((halves, QUAD * mid, lon + 2 * LANE), BF16),
            pltpu.VMEM((halves, QUAD * mid, lon), BF16),
            pltpu.VMEM((ITERS, levels, lat, lon), F32),
            pltpu.VMEM((ITERS, levels, rest, 8, LANE), F32),
            pltpu.VMEM((levels, 8, LANE), F32),
            pltpu.VMEM((ITERS, lat // 8, 8 * levels, lon), F32),
            pltpu.VMEM((2 * rows, lon), BF16),
            pltpu.VMEM((ITERS, 8, LANE), F32),
            pltpu.VMEM((ITERS, n_band - 1, 8, LANE), F32),
            pltpu.VMEM((ITERS, 8, LANE), F32),
            pltpu.VMEM((ITERS, rest, 8, LANE), F32),
            dma((2,)),
            dma((2,)), dma((2,)),
            dma((2,)), dma((2,)),
            dma((ITERS, 2)), dma((ITERS, 2)),
            dma((ITERS, levels)), dma((ITERS, levels)),
            dma((ITERS,)), dma((ITERS,)),
            dma((ITERS, 2)), dma((ITERS, 2)),
        ],
        compiler_params=pltpu.CompilerParams(
            collective_id=0, has_side_effects=True, vmem_limit_bytes=52 * 1024 * 1024
        ),
    )(root_ranks, ensemble, variance, obs_index, obs_value, obs_error)


def solution(mesh):
    in_specs = (
        P("member", None, "band", None),
        P(None, "band", None),
        P("member", "band"),
        P("member", "band"),
        P("member", "band"),
        P(),
    )
    body = functools.partial(local, mesh.shape["band"], mesh.shape["member"])
    return jax.shard_map(body, mesh=mesh, in_specs=in_specs, out_specs=P(None, "band", None), check_vma=False)
```

```python
import functools
import math

import jax
import jax.numpy as jnp
from jax import lax
from jax.experimental import pallas as pl
from jax.experimental.pallas import tpu as pltpu
from jax.sharding import PartitionSpec as P

HALF = 8
ITERS = 2
LANE = 128
HALO = 2 * HALF
BLK = 256
QUAD = 4
GROUP = 4

huber_edge = 1.5
ensemble_share = 0.75
static_share = 0.25

F32 = jnp.float32
BF16 = jnp.bfloat16


def taps(distance, keep):
    raw = [math.exp(-0.5 * (k / (0.5 * HALF)) ** 2) for k in range(-HALF, HALF + 1)]
    norm = math.sqrt(sum(r * r for r in raw))
    scaled = distance.astype(F32) / (0.5 * HALF)
    entry = jnp.exp(-0.5 * scaled * scaled) / norm
    keep = keep & (jnp.abs(distance) <= HALF)
    return jnp.where(keep, entry, 0.0).astype(BF16)


def iota(shape, dim):
    return lax.broadcasted_iota(jnp.int32, shape, dim)


def split(x):
    hi = x.astype(BF16).astype(F32)
    return hi, x - hi


def kernel(
    n_band, n_member, members_here, levels, lat, lon,
    root_hbm, ens_ref, var_ref, idx_hbm, val_hbm, err_hbm, out_ref,
    root_ref, idx_ref, val_ref, err_ref,
    ext, wlon, lat1, lat2, send_obs, got_obs, obs, hot, lhs, lhs2, reached, grad2, gpad,
    xpad, ypad, zpad, vpad, spread, arrived, varp, direc, direc_lo,
    sums, band_sums, total_sums, member_sums,
    own_sem, ens_send, ens_recv, obs_send, obs_recv, halo_send, halo_recv,
    rs_send, rs_recv, ag_send, ag_recv, lo_send, lo_recv, sc_send, sc_recv,
):
    me = lax.axis_index("member")
    band = lax.axis_index("band")
    rest = n_member - 1
    cols = lon // LANE
    wide = lat + 2 * HALO
    mid = lat + 2 * HALF
    rows = levels * lat
    up = lax.rem(band + 1, n_band)
    down = lax.rem(band + n_band - 1, n_band)
    my_row = pl.multiple_of((me // cols) * 8, 8)
    my_col = pl.multiple_of((me % cols) * LANE, LANE)

    def remote(src, dst, send, recv, to_band, to_member):
        return pltpu.make_async_remote_copy(
            src_ref=src, dst_ref=dst, send_sem=send, recv_sem=recv,
            device_id=(to_band, to_member), device_id_type=pl.DeviceIdType.MESH,
        )

    def drain(ref, sem):
        pltpu.make_async_copy(ref, ref, sem).wait()

    def to_members(start):
        def body(k, carry):
            start(k, lax.rem(me + k, n_member))
            return carry
        lax.fori_loop(1, n_member, body, 0)

    loads = [
        pltpu.make_async_copy(src, dst, own_sem.at[2 + i])
        for i, (src, dst) in enumerate(
            ((root_hbm, root_ref), (idx_hbm, idx_ref), (val_hbm, val_ref), (err_hbm, err_ref))
        )
    ]
    for load in loads:
        load.start()

    barrier = pltpu.get_barrier_semaphore()

    def greet_member(k, peer):
        pl.semaphore_signal(barrier, inc=1, device_id=(band, peer), device_id_type=pl.DeviceIdType.MESH)

    to_members(greet_member)

    def greet_band(k, carry):
        pl.semaphore_signal(
            barrier, inc=1, device_id=(lax.rem(band + k, n_band), me), device_id_type=pl.DeviceIdType.MESH
        )
        return carry

    lax.fori_loop(1, n_band, greet_band, 0)

    own = pltpu.make_async_copy(ens_ref, ext.at[:, :, pl.ds(HALO, lat), :], own_sem.at[0])
    own.start()
    own_var = pltpu.make_async_copy(
        var_ref.at[:, pl.ds(my_row, 8), pl.ds(my_col, LANE)], varp, own_sem.at[1]
    )
    own_var.start()

    for load in loads:
        load.wait()

    flags = [(root_ref[it] == me).astype(F32) for it in range(ITERS)]
    for j in range(n_member):
        at = pl.ds(j * LANE, LANE)
        parts = [idx_ref[0:1, at].astype(F32), val_ref[0:1, at], err_ref[0:1, at]]
        lines = [part * flags[it] for it in range(ITERS) for part in parts]
        send_obs[j] = jnp.concatenate(lines + [jnp.zeros((2, LANE), F32)], axis=0)

    pl.semaphore_wait(barrier, n_member - 1 + n_band - 1)

    to_members(
        lambda k, peer: remote(
            send_obs.at[peer], got_obs.at[k - 1], obs_send.at[0], obs_recv.at[0], band, peer
        ).start()
    )
    ens_up = remote(
        ens_ref.at[:, :, pl.ds(lat - HALO, HALO), :], ext.at[:, :, pl.ds(0, HALO), :],
        ens_send.at[0], ens_recv.at[0], up, me,
    )
    ens_down = remote(
        ens_ref.at[:, :, pl.ds(0, HALO), :], ext.at[:, :, pl.ds(HALO + lat, HALO), :],
        ens_send.at[1], ens_recv.at[1], down, me,
    )
    ens_up.start()
    ens_down.start()

    shape = (2 * BLK, BLK)
    wlon[...] = taps(iota(shape, 1) - iota(shape, 0) + LANE, iota(shape, 0) >= 0)
    shape = (QUAD * mid, QUAD * wide)
    target, source = iota(shape, 0), iota(shape, 1)
    row_out = band * lat - HALF + target % mid
    row_in = band * lat - HALO + source % wide
    all_rows = n_band * lat
    lat1[...] = taps(
        row_in - row_out,
        (target // mid == source // wide)
        & (row_out >= 0) & (row_out < all_rows) & (row_in >= 0) & (row_in < all_rows),
    )
    shape = (QUAD * lat, QUAD * mid)
    target, source = iota(shape, 0), iota(shape, 1)
    lat2[...] = taps(source % mid - HALF - target % lat, target // lat == source // mid)

    drain(got_obs, obs_recv.at[0])
    obs[me] = send_obs[me] + jnp.sum(got_obs[...], axis=0)
    to_members(
        lambda k, peer: remote(
            obs.at[me], obs.at[me], obs_send.at[1], obs_recv.at[1], band, peer
        ).start()
    )
    drain(got_obs, obs_recv.at[1])

    groups = n_member // GROUP
    width = GROUP * LANE

    def line(g, which):
        return jnp.concatenate([obs[g * GROUP + j, which : which + 1, :] for j in range(GROUP)], axis=1)

    def columns(g):
        return pl.ds(pl.multiple_of(g * width, width), width)

    def each_group(step):
        def body(g, carry):
            step(g)
            return carry
        lax.fori_loop(0, groups, body, 0)

    def build_hot(it):
        def step(g):
            column = line(g, 3 * it).astype(jnp.int32) % lon
            for r in range(0, lon, LANE):
                hit = iota((LANE, width), 0) + r == column
                hot[r : r + LANE, columns(g)] = jnp.where(hit, 1.0, 0.0).astype(BF16)
        each_group(step)

    nt = (((1,), (1,)), ((), ()))

    def gather(it):
        field = direc[it - 1].reshape(rows, lon)

        def step(g):
            row = line(g, 3 * it).astype(jnp.int32) // lon
            level, in_level = row // lat, row % lat
            line_of = (in_level // 8) * (8 * levels) + level * 8 + in_level % 8
            found = jnp.dot(field, hot[:, columns(g)], preferred_element_type=F32)
            found = jnp.where(iota((rows, width), 0) == line_of, found, 0.0)
            reached[:, columns(g)] = jnp.sum(found, axis=0, keepdims=True)
        each_group(step)

    def build_terms(it, scale):
        def step(g):
            values = line(g, 3 * it + 1)
            errors = line(g, 3 * it + 2)
            row = line(g, 3 * it).astype(jnp.int32) // lon
            departure = values
            if it > 0:
                departure = values - scale * reached[:, columns(g)]
            weight = huber_edge / jnp.maximum(jnp.abs(departure / errors), huber_edge)
            square = errors * errors
            hit = iota((rows, width), 0) == row
            for i, part in enumerate(split(weight * departure / square)):
                lhs[i * rows : (i + 1) * rows, columns(g)] = jnp.where(hit, part, 0.0).astype(BF16)
            mine = iota((8 * levels, width), 0)
            hit = (mine // 8) * lat + my_row + mine % 8 == row
            for i, part in enumerate(split(weight / square)):
                a = i * 8 * levels
                lhs2[a : a + 8 * levels, columns(g)] = jnp.where(hit, part, 0.0).astype(BF16)
        each_group(step)

    def halos(it, b):
        at = pl.ds(b * BLK, BLK)
        return [
            remote(
                gpad.at[it, :, pl.ds(lat, HALO), at], gpad.at[it, :, pl.ds(0, HALO), at],
                halo_send.at[it, 0, b], halo_recv.at[it, 0, b], up, me,
            ),
            remote(
                gpad.at[it, :, pl.ds(HALO, HALO), at], gpad.at[it, :, pl.ds(HALO + lat, HALO), at],
                halo_send.at[it, 1, b], halo_recv.at[it, 1, b], down, me,
            ),
        ]

    def scatter(it):
        for b in range(lon // BLK):
            at = slice(b * BLK, (b + 1) * BLK)
            both = lax.dot_general(lhs[...], hot[at, :], nt, preferred_element_type=F32)
            block = both[:rows] + both[rows:]
            gpad[it, :, HALO : HALO + lat, at] = block.reshape(levels, lat, BLK)
            for copy in halos(it, b):
                copy.start()
        grad2[...] = lax.dot_general(
            lhs2[...], hot[pl.ds(my_col, LANE), :], nt, preferred_element_type=F32
        )

    def lon_filter(padded, store):
        for c in range(0, lon, BLK):
            at = slice(c, c + BLK)
            store(at, jnp.dot(padded[:, c : c + 2 * BLK], wlon[...], preferred_element_type=F32).astype(BF16))

    def put_padded(ref, at, block):
        ref[:, LANE + at.start : LANE + at.stop] = block
        if at.start == 0:
            ref[:, LANE + lon :] = block[:, :LANE]
        if at.stop == lon:
            ref[:, :LANE] = block[:, block.shape[1] - LANE :]

    def lon_of_rows(it, level, at_rows):
        for c in range(0, lon, BLK):
            at = slice(c, c + BLK)
            blocks = []
            for part in at_rows:
                mixed = ext[:, level, part, at].astype(F32) * gpad[it, level, part, at][None]
                blocks.append(mixed.astype(BF16).reshape(members_here * (part.stop - part.start), BLK))
            put_padded(xpad, at, jnp.concatenate(blocks, axis=0))

        def store(at, block):
            a = 0
            for part in at_rows:
                length = part.stop - part.start
                size = members_here * length
                ypad[level, :, part, at] = block[a : a + size].reshape(members_here, length, BLK)
                a += size

        lon_filter(xpad, store)

    def filters(it, level):
        lon_of_rows(it, level, (slice(0, HALO), slice(HALO + lat, wide)))
        for h in range(members_here // QUAD):
            who = slice(h * QUAD, (h + 1) * QUAD)
            zs, vs = zpad.at[h], vpad.at[h]
            for c in range(0, lon, BLK):
                at = slice(c, c + BLK)
                first = ypad[level, who, :, at].reshape(QUAD * wide, BLK)
                put_padded(zs, at, jnp.dot(lat1[...], first, preferred_element_type=F32).astype(BF16))

            def store_v(at, block):
                vs[:, at] = block

            lon_filter(zs, store_v)
            for c in range(0, lon, BLK):
                at = slice(c, c + BLK)
                second = jnp.dot(lat2[...], vs[:, at], preferred_element_type=F32).reshape(QUAD, lat, BLK)
                part = jnp.sum(ext[who, level, HALO : HALO + lat, at].astype(F32) * second, axis=0)
                if h == 0:
                    spread[it, level, :, at] = part
                else:
                    spread[it, level, :, at] += part

    steps = []
    fields = []
    build_hot(0)
    for it in range(ITERS):
        build_terms(it, steps[-1] if steps else None)
        scatter(it)
        if it == 0:
            own.wait()
            own_var.wait()

        def middle(level, carry):
            lon_of_rows(it, level, (slice(HALO, HALO + lat),))
            return carry

        lax.fori_loop(0, levels, middle, 0)
        if it == 0:
            ens_up.wait()
            ens_down.wait()
        for b in range(lon // BLK):
            for copy in halos(it, b):
                copy.wait()

        def level_body(level, carry):
            filters(it, level)

            def send(k, peer):
                row = pl.multiple_of((peer // cols) * 8, 8)
                col = pl.multiple_of((peer % cols) * LANE, LANE)
                remote(
                    spread.at[it, level, pl.ds(row, 8), pl.ds(col, LANE)], arrived.at[it, level, k - 1],
                    rs_send.at[it, level], rs_recv.at[it, level], band, peer,
                ).start()

            to_members(send)
            return carry

        lax.fori_loop(0, levels, level_body, 0)

        along = jnp.zeros((8, LANE), F32)
        back = jnp.zeros((8, LANE), F32)
        curve = jnp.zeros((8, LANE), F32)
        pieces = []
        for level in range(levels):
            drain(arrived.at[it, level], rs_recv.at[it, level])
            summed = spread[it, level, pl.ds(my_row, 8), pl.ds(my_col, LANE)] + jnp.sum(arrived[it, level], axis=0)
            g = gpad[it, level, pl.ds(HALO + my_row, 8), pl.ds(my_col, LANE)]
            d = ensemble_share * summed / (members_here * n_member - 1) + static_share * varp[level] * g
            a = level * 8
            c = grad2[a : a + 8, :] + grad2[a + 8 * levels : a + 8 * levels + 8, :]
            along += g * d
            curve += c * d * d
            if it > 0:
                back += fields[-1][level] * g
            pieces.append(d)
        sums[it] = jnp.concatenate(
            [jnp.sum(x, axis=0, keepdims=True) for x in (along, back, curve)] + [jnp.zeros((5, LANE), F32)], axis=0
        )

        def send_sums(k, carry):
            remote(
                sums.at[it], band_sums.at[it, k - 1], sc_send.at[it, 0], sc_recv.at[it, 0],
                lax.rem(band + k, n_band), me,
            ).start()
            return carry

        lax.fori_loop(1, n_band, send_sums, 0)

        hi, lo = split(jnp.concatenate(pieces, axis=0))
        direc[it, me // cols, :, pl.ds(my_col, LANE)] = hi.astype(BF16)

        def send_piece(k, peer):
            piece = direc.at[it, me // cols, :, pl.ds(my_col, LANE)]
            remote(piece, piece, ag_send.at[it], ag_recv.at[it], band, peer).start()

        to_members(send_piece)
        if it + 1 < ITERS:
            build_hot(it + 1)
        drain(band_sums.at[it], sc_recv.at[it, 0])
        total_sums[it] = sums[it] + jnp.sum(band_sums[it], axis=0)
        to_members(
            lambda k, peer: remote(
                total_sums.at[it], member_sums.at[it, k - 1], sc_send.at[it, 1], sc_recv.at[it, 1], band, peer
            ).start()
        )
        drain(arrived.at[it, pl.ds(0, levels // 2)], ag_recv.at[it])
        if it + 1 < ITERS:
            gather(it + 1)
        drain(member_sums.at[it], sc_recv.at[it, 1])
        total = jnp.sum(total_sums[it] + jnp.sum(member_sums[it], axis=0), axis=1, keepdims=True)
        step = (total[0:1] - total[1:2]) / (total[0:1] + total[2:3])
        steps.append(step)
        fields.append([step * d for d in pieces])
        if it + 1 < ITERS:
            direc_lo[me // cols, :, pl.ds(my_col, LANE)] = lo.astype(BF16)

            def send_lo(k, peer):
                piece = direc_lo.at[me // cols, :, pl.ds(my_col, LANE)]
                remote(piece, piece, lo_send, lo_recv, band, peer).start()

            to_members(send_lo)

    drain(arrived.at[0, pl.ds(0, levels // 2)], lo_recv)
    for r in range(lat // 8):
        first = direc[0, r].astype(F32) + direc_lo[r].astype(F32)
        moved = steps[0] * first + steps[1] * direc[1, r].astype(F32)
        for level in range(levels):
            out_ref[level, r * 8 : r * 8 + 8, :] = moved[level * 8 : level * 8 + 8]

    drain(got_obs, obs_send.at[0])
    drain(got_obs, obs_send.at[1])
    for it in range(ITERS):
        for level in range(levels):
            drain(arrived.at[it, level], rs_send.at[it, level])
        drain(arrived.at[it, pl.ds(0, levels // 2)], ag_send.at[it])
        drain(band_sums.at[it], sc_send.at[it, 0])
        drain(member_sums.at[it], sc_send.at[it, 1])
    drain(arrived.at[0, pl.ds(0, levels // 2)], lo_send)


def local(n_band, n_member, ensemble, variance, obs_index, obs_value, obs_error, root_ranks):
    members_here, levels, lat, lon = ensemble.shape
    wide, mid, rows = lat + 2 * HALO, lat + 2 * HALF, levels * lat
    halves = members_here // QUAD
    rest = n_member - 1
    dma = pltpu.SemaphoreType.DMA
    vmem = pl.BlockSpec(memory_space=pltpu.VMEM)
    hbm = pl.BlockSpec(memory_space=pltpu.HBM)
    return pl.pallas_call(
        functools.partial(kernel, n_band, n_member, members_here, levels, lat, lon),
        out_shape=jax.ShapeDtypeStruct((levels, lat, lon), F32),
        in_specs=[hbm] * 6,
        out_specs=vmem,
        scratch_shapes=[
            pltpu.SMEM((ITERS,), jnp.int32),
            pltpu.VMEM((1, n_member * LANE), jnp.int32),
            pltpu.VMEM((1, n_member * LANE), F32),
            pltpu.VMEM((1, n_member * LANE), F32),
            pltpu.VMEM((members_here, levels, wide, lon), BF16),
            pltpu.VMEM((2 * BLK, BLK), BF16),
            pltpu.VMEM((QUAD * mid, QUAD * wide), BF16),
            pltpu.VMEM((QUAD * lat, QUAD * mid), BF16),
            pltpu.VMEM((n_member, 8, LANE), F32),
            pltpu.VMEM((rest, 8, LANE), F32),
            pltpu.VMEM((n_member, 8, LANE), F32),
            pltpu.VMEM((lon, n_member * LANE), BF16),
            pltpu.VMEM((2 * rows, n_member * LANE), BF16),
            pltpu.VMEM((2 * 8 * levels, n_member * LANE), BF16),
            pltpu.VMEM((1, n_member * LANE), F32),
            pltpu.VMEM((2 * 8 * levels, LANE), F32),
            pltpu.VMEM((ITERS, levels, wide, lon), F32),
            pltpu.VMEM((members_here * lat, lon + 2 * LANE), BF16),
            pltpu.VMEM((levels, members_here, wide, lon), BF16),
            pltpu.VMEM((halves, QUAD * mid, lon + 2 * LANE), BF16),
            pltpu.VMEM((halves, QUAD * mid, lon), BF16),
            pltpu.VMEM((ITERS, levels, lat, lon), F32),
            pltpu.VMEM((ITERS, levels, rest, 8, LANE), F32),
            pltpu.VMEM((levels, 8, LANE), F32),
            pltpu.VMEM((ITERS, lat // 8, 8 * levels, lon), BF16),
            pltpu.VMEM((lat // 8, 8 * levels, lon), BF16),
            pltpu.VMEM((ITERS, 8, LANE), F32),
            pltpu.VMEM((ITERS, n_band - 1, 8, LANE), F32),
            pltpu.VMEM((ITERS, 8, LANE), F32),
            pltpu.VMEM((ITERS, rest, 8, LANE), F32),
            dma((6,)),
            dma((2,)), dma((2,)),
            dma((2,)), dma((2,)),
            dma((ITERS, 2, lon // BLK)), dma((ITERS, 2, lon // BLK)),
            dma((ITERS, levels)), dma((ITERS, levels)),
            dma((ITERS,)), dma((ITERS,)),
            dma, dma,
            dma((ITERS, 2)), dma((ITERS, 2)),
        ],
        compiler_params=pltpu.CompilerParams(
            collective_id=0, has_side_effects=True, vmem_limit_bytes=65500 * 1024
        ),
    )(root_ranks, ensemble, variance, obs_index, obs_value, obs_error)


def solution(mesh):
    in_specs = (
        P("member", None, "band", None),
        P(None, "band", None),
        P("member", "band"),
        P("member", "band"),
        P("member", "band"),
        P(),
    )
    body = functools.partial(local, mesh.shape["band"], mesh.shape["member"])
    return jax.shard_map(body, mesh=mesh, in_specs=in_specs, out_specs=P(None, "band", None), check_vma=False)
```

```python
import functools
import math

import jax
import jax.numpy as jnp
from jax import lax
from jax.experimental import pallas as pl
from jax.experimental.pallas import tpu as pltpu
from jax.sharding import PartitionSpec as P

HALF = 8
ITERS = 2
LANE = 128
HALO = 2 * HALF
BLK = 256
QUAD = 4
GROUP = 4

huber_edge = 1.5
ensemble_share = 0.75
static_share = 0.25

F32 = jnp.float32
BF16 = jnp.bfloat16


def taps(distance, keep):
    raw = [math.exp(-0.5 * (k / (0.5 * HALF)) ** 2) for k in range(-HALF, HALF + 1)]
    norm = math.sqrt(sum(r * r for r in raw))
    scaled = distance.astype(F32) / (0.5 * HALF)
    entry = jnp.exp(-0.5 * scaled * scaled) / norm
    keep = keep & (jnp.abs(distance) <= HALF)
    return jnp.where(keep, entry, 0.0).astype(BF16)


def iota(shape, dim):
    return lax.broadcasted_iota(jnp.int32, shape, dim)


def split(x):
    hi = x.astype(BF16).astype(F32)
    return hi, x - hi


def kernel(
    n_band, n_member, members_here, levels, lat, lon,
    root_hbm, ens_ref, var_ref, idx_hbm, val_hbm, err_hbm, out_ref,
    root_ref, idx_ref, val_ref, err_ref,
    ext, wlon, lat1, lat2, send_obs, got_obs, obs, hot, lhs, lhs2, reached, grad2, gpad,
    xpad, ypad, zpad, vpad, spread, from_x, of_x, from_z, arrived, varp, direc, direc_lo,
    sums, near_sums, total_sums, far_sums,
    own_sem, ens_send, ens_recv, obs_send, obs_recv, halo_send, halo_recv,
    x_send, x_recv, z_send, z_recv, rs_send, rs_recv, ag_send, ag_recv, lo_send, lo_recv, sc_send, sc_recv,
):
    me = lax.axis_index("member")
    band = lax.axis_index("band")
    rest = n_member - 1
    cols = lon // LANE
    wide = lat + 2 * HALO
    mid = lat + 2 * HALF
    rows = levels * lat
    up = lax.rem(band + 1, n_band)
    down = lax.rem(band + n_band - 1, n_band)
    my_x, my_z = me // cols, me % cols
    n_x, n_z, n_y = n_member // cols, cols, n_band // 2
    my_y, core = band // 2, band % 2
    my_row = pl.multiple_of(my_x * 8, 8)
    my_col = pl.multiple_of(my_z * LANE, LANE)
    last = levels - 1

    def remote(src, dst, send, recv, to_band, to_member):
        return pltpu.make_async_remote_copy(
            src_ref=src, dst_ref=dst, send_sem=send, recv_sem=recv,
            device_id=(to_band, to_member), device_id_type=pl.DeviceIdType.MESH,
        )

    def drain(ref, sem):
        pltpu.make_async_copy(ref, ref, sem).wait()

    def each(first, stop, start):
        def body(k, carry):
            start(k)
            return carry
        lax.fori_loop(first, stop, body, 0)

    def to_members(start):
        each(1, n_member, lambda k: start(k, lax.rem(me + k, n_member)))

    def near(k):
        index = lax.rem(core * n_z + my_z + k, 2 * n_z)
        return my_y * 2 + index // n_z, my_x * n_z + index % n_z

    def far(k):
        index = lax.rem(my_x * n_y + my_y + k, n_x * n_y)
        return (index % n_y) * 2 + core, (index // n_y) * n_z + my_z

    loads = [
        pltpu.make_async_copy(src, dst, own_sem.at[2 + i])
        for i, (src, dst) in enumerate(
            ((root_hbm, root_ref), (idx_hbm, idx_ref), (val_hbm, val_ref), (err_hbm, err_ref))
        )
    ]
    for load in loads:
        load.start()

    barrier = pltpu.get_barrier_semaphore()

    def greet(to_band, to_member):
        pl.semaphore_signal(
            barrier, inc=1, device_id=(to_band, to_member), device_id_type=pl.DeviceIdType.MESH
        )

    to_members(lambda k, peer: greet(band, peer))
    each(0, n_z, lambda k: greet(my_y * 2 + 1 - core, my_x * n_z + k))

    def greet_plane(k):
        greet(lax.rem(my_y + 1 + k // n_x, n_y) * 2 + core, (k % n_x) * n_z + my_z)

    greeted = n_x * (n_y - 1)
    each(0, greeted, greet_plane)
    greet(lax.rem(band + n_band + 2 * core - 1, n_band), me)
    greeted += n_member - 1 + n_z + 1

    own = pltpu.make_async_copy(ens_ref, ext.at[:, :, pl.ds(HALO, lat), :], own_sem.at[0])
    own.start()
    own_var = pltpu.make_async_copy(
        var_ref.at[:, pl.ds(my_row, 8), pl.ds(my_col, LANE)], varp, own_sem.at[1]
    )
    own_var.start()

    for load in loads:
        load.wait()

    flags = [(root_ref[it] == me).astype(F32) for it in range(ITERS)]
    for j in range(n_member):
        at = pl.ds(j * LANE, LANE)
        parts = [idx_ref[0:1, at].astype(F32), val_ref[0:1, at], err_ref[0:1, at]]
        lines = [part * flags[it] for it in range(ITERS) for part in parts]
        send_obs[j] = jnp.concatenate(lines + [jnp.zeros((2, LANE), F32)], axis=0)

    pl.semaphore_wait(barrier, greeted)

    to_members(
        lambda k, peer: remote(
            send_obs.at[peer], got_obs.at[k - 1], obs_send.at[0], obs_recv.at[0], band, peer
        ).start()
    )
    ens_up = remote(
        ens_ref.at[:, :, pl.ds(lat - HALO, HALO), :], ext.at[:, :, pl.ds(0, HALO), :],
        ens_send.at[0], ens_recv.at[0], up, me,
    )
    ens_down = remote(
        ens_ref.at[:, :, pl.ds(0, HALO), :], ext.at[:, :, pl.ds(HALO + lat, HALO), :],
        ens_send.at[1], ens_recv.at[1], down, me,
    )
    ens_up.start()
    ens_down.start()

    shape = (2 * BLK, BLK)
    wlon[...] = taps(iota(shape, 1) - iota(shape, 0) + LANE, iota(shape, 0) >= 0)
    shape = (QUAD * mid, QUAD * wide)
    target, source = iota(shape, 0), iota(shape, 1)
    row_out = band * lat - HALF + target % mid
    row_in = band * lat - HALO + source % wide
    all_rows = n_band * lat
    lat1[...] = taps(
        row_in - row_out,
        (target // mid == source // wide)
        & (row_out >= 0) & (row_out < all_rows) & (row_in >= 0) & (row_in < all_rows),
    )
    shape = (QUAD * lat, QUAD * mid)
    target, source = iota(shape, 0), iota(shape, 1)
    lat2[...] = taps(source % mid - HALF - target % lat, target // lat == source // mid)

    drain(got_obs, obs_recv.at[0])
    obs[me] = send_obs[me] + jnp.sum(got_obs[...], axis=0)
    to_members(
        lambda k, peer: remote(
            obs.at[me], obs.at[me], obs_send.at[1], obs_recv.at[1], band, peer
        ).start()
    )
    drain(got_obs, obs_recv.at[1])

    groups = n_member // GROUP
    width = GROUP * LANE

    def line(g, which):
        return jnp.concatenate([obs[g * GROUP + j, which : which + 1, :] for j in range(GROUP)], axis=1)

    def columns(g):
        return pl.ds(pl.multiple_of(g * width, width), width)

    def each_group(step):
        def body(g, carry):
            step(g)
            return carry
        lax.fori_loop(0, groups, body, 0)

    def build_hot(it):
        def step(g):
            column = line(g, 3 * it).astype(jnp.int32) % lon
            for r in range(0, lon, LANE):
                hit = iota((LANE, width), 0) + r == column
                hot[r : r + LANE, columns(g)] = jnp.where(hit, 1.0, 0.0).astype(BF16)
        each_group(step)

    nt = (((1,), (1,)), ((), ()))

    def gather(it):
        field = direc[it - 1].reshape(rows, lon)

        def step(g):
            row = line(g, 3 * it).astype(jnp.int32) // lon
            level, in_level = row // lat, row % lat
            line_of = (in_level // 8) * (8 * levels) + level * 8 + in_level % 8
            found = jnp.dot(field, hot[:, columns(g)], preferred_element_type=F32)
            found = jnp.where(iota((rows, width), 0) == line_of, found, 0.0)
            reached[:, columns(g)] = jnp.sum(found, axis=0, keepdims=True)
        each_group(step)

    def build_terms(it, scale):
        def step(g):
            values = line(g, 3 * it + 1)
            errors = line(g, 3 * it + 2)
            row = line(g, 3 * it).astype(jnp.int32) // lon
            departure = values
            if it > 0:
                departure = values - scale * reached[:, columns(g)]
            weight = huber_edge / jnp.maximum(jnp.abs(departure / errors), huber_edge)
            square = errors * errors
            hit = iota((rows, width), 0) == row
            for i, part in enumerate(split(weight * departure / square)):
                lhs[i * rows : (i + 1) * rows, columns(g)] = jnp.where(hit, part, 0.0).astype(BF16)
            mine = iota((8 * levels, width), 0)
            hit = (mine // 8) * lat + my_row + mine % 8 == row
            for i, part in enumerate(split(weight / square)):
                a = i * 8 * levels
                lhs2[a : a + 8 * levels, columns(g)] = jnp.where(hit, part, 0.0).astype(BF16)
        each_group(step)

    def halos(it, b):
        at = pl.ds(b * BLK, BLK)
        return [
            remote(
                gpad.at[it, :, pl.ds(lat, HALO), at], gpad.at[it, :, pl.ds(0, HALO), at],
                halo_send.at[it, 0, b], halo_recv.at[it, 0, b], up, me,
            ),
            remote(
                gpad.at[it, :, pl.ds(HALO, HALO), at], gpad.at[it, :, pl.ds(HALO + lat, HALO), at],
                halo_send.at[it, 1, b], halo_recv.at[it, 1, b], down, me,
            ),
        ]

    def scatter(it):
        for b in range(lon // BLK):
            at = slice(b * BLK, (b + 1) * BLK)
            both = lax.dot_general(lhs[...], hot[at, :], nt, preferred_element_type=F32)
            block = both[:rows] + both[rows:]
            gpad[it, :, HALO : HALO + lat, at] = block.reshape(levels, lat, BLK)
            for copy in halos(it, b):
                copy.start()
        grad2[...] = lax.dot_general(
            lhs2[...], hot[pl.ds(my_col, LANE), :], nt, preferred_element_type=F32
        )

    def lon_filter(padded, store):
        for c in range(0, lon, BLK):
            at = slice(c, c + BLK)
            store(at, jnp.dot(padded[:, c : c + 2 * BLK], wlon[...], preferred_element_type=F32).astype(BF16))

    def put_padded(ref, at, block):
        ref[:, LANE + at.start : LANE + at.stop] = block
        if at.start == 0:
            ref[:, LANE + lon :] = block[:, :LANE]
        if at.stop == lon:
            ref[:, :LANE] = block[:, block.shape[1] - LANE :]

    def lon_of_rows(it, level, at_rows):
        for c in range(0, lon, BLK):
            at = slice(c, c + BLK)
            blocks = []
            for part in at_rows:
                mixed = ext[:, level, part, at].astype(F32) * gpad[it, level, part, at][None]
                blocks.append(mixed.astype(BF16).reshape(members_here * (part.stop - part.start), BLK))
            put_padded(xpad, at, jnp.concatenate(blocks, axis=0))

        def store(at, block):
            a = 0
            for part in at_rows:
                length = part.stop - part.start
                size = members_here * length
                ypad[level, :, part, at] = block[a : a + size].reshape(members_here, length, BLK)
                a += size

        lon_filter(xpad, store)

    def filters(it, level):
        lon_of_rows(it, level, (slice(0, HALO), slice(HALO + lat, wide)))
        for h in range(members_here // QUAD):
            who = slice(h * QUAD, (h + 1) * QUAD)
            zs, vs = zpad.at[h], vpad.at[h]
            for c in range(0, lon, BLK):
                at = slice(c, c + BLK)
                first = ypad[level, who, :, at].reshape(QUAD * wide, BLK)
                put_padded(zs, at, jnp.dot(lat1[...], first, preferred_element_type=F32).astype(BF16))

            def store_v(at, block):
                vs[:, at] = block

            lon_filter(zs, store_v)
            for c in range(0, lon, BLK):
                at = slice(c, c + BLK)
                second = jnp.dot(lat2[...], vs[:, at], preferred_element_type=F32).reshape(QUAD, lat, BLK)
                part = jnp.sum(ext[who, level, HALO : HALO + lat, at].astype(F32) * second, axis=0)
                if h == 0:
                    spread[it, level, :, at] = part
                else:
                    spread[it, level, :, at] += part

    steps = []
    fields = []
    build_hot(0)
    for it in range(ITERS):
        build_terms(it, steps[-1] if steps else None)
        scatter(it)
        if it == 0:
            own.wait()
            own_var.wait()

        def middle(level, carry):
            lon_of_rows(it, level, (slice(HALO, HALO + lat),))
            return carry

        lax.fori_loop(0, levels, middle, 0)
        if it == 0:
            ens_up.wait()
            ens_down.wait()
        for b in range(lon // BLK):
            for copy in halos(it, b):
                copy.wait()

        def level_body(level, carry):
            filters(it, level)

            @pl.when(level < last)
            def _():
                def send_x(k):
                    to_x = lax.rem(my_x + k, n_x)
                    row = pl.multiple_of(to_x * 8, 8)
                    remote(
                        spread.at[it, level, pl.ds(row, 8), :], from_x.at[it, level, k - 1],
                        x_send.at[it, level], x_recv.at[it, level], band, to_x * n_z + my_z,
                    ).start()

                each(1, n_x, send_x)

            @pl.when(level == last)
            def _():
                def send(k, peer):
                    row = pl.multiple_of((peer // n_z) * 8, 8)
                    col = pl.multiple_of((peer % n_z) * LANE, LANE)
                    remote(
                        spread.at[it, last, pl.ds(row, 8), pl.ds(col, LANE)], arrived.at[it, k - 1],
                        rs_send.at[it], rs_recv.at[it], band, peer,
                    ).start()

                to_members(send)
            return carry

        lax.fori_loop(0, levels, level_body, 0)

        def pass_on(level):
            drain(from_x.at[it, level], x_recv.at[it, level])
            of_x[it, level] = spread[it, level, pl.ds(my_row, 8), :] + jnp.sum(from_x[it, level], axis=0)

            def send_z(k):
                to_z = lax.rem(my_z + k, n_z)
                col = pl.multiple_of(to_z * LANE, LANE)
                remote(
                    of_x.at[it, level, :, pl.ds(col, LANE)], from_z.at[it, level, k - 1],
                    z_send.at[it, level], z_recv.at[it, level], band, my_x * n_z + to_z,
                ).start()

            each(1, n_z, send_z)

        each(0, last, pass_on)

        along = jnp.zeros((8, LANE), F32)
        back = jnp.zeros((8, LANE), F32)
        curve = jnp.zeros((8, LANE), F32)
        pieces = []
        for level in range(levels):
            if level < last:
                drain(from_z.at[it, level], z_recv.at[it, level])
                summed = of_x[it, level, :, pl.ds(my_col, LANE)] + jnp.sum(from_z[it, level], axis=0)
            else:
                drain(arrived.at[it], rs_recv.at[it])
                summed = spread[it, level, pl.ds(my_row, 8), pl.ds(my_col, LANE)] + jnp.sum(arrived[it], axis=0)
            g = gpad[it, level, pl.ds(HALO + my_row, 8), pl.ds(my_col, LANE)]
            d = ensemble_share * summed / (members_here * n_member - 1) + static_share * varp[level] * g
            a = level * 8
            c = grad2[a : a + 8, :] + grad2[a + 8 * levels : a + 8 * levels + 8, :]
            along += g * d
            curve += c * d * d
            if it > 0:
                back += fields[-1][level] * g
            pieces.append(d)
        sums[it] = jnp.concatenate(
            [jnp.sum(x, axis=0, keepdims=True) for x in (along, back, curve)] + [jnp.zeros((5, LANE), F32)], axis=0
        )

        def send_sums(k):
            remote(sums.at[it], near_sums.at[it, k - 1], sc_send.at[it, 0], sc_recv.at[it, 0], *near(k)).start()

        each(1, 2 * n_z, send_sums)
        hi, lo = split(jnp.concatenate(pieces, axis=0))
        direc[it, my_x, :, pl.ds(my_col, LANE)] = hi.astype(BF16)

        def send_piece(k, peer):
            piece = direc.at[it, my_x, :, pl.ds(my_col, LANE)]
            remote(piece, piece, ag_send.at[it], ag_recv.at[it], band, peer).start()

        to_members(send_piece)
        if it + 1 < ITERS:
            build_hot(it + 1)
        drain(near_sums.at[it], sc_recv.at[it, 0])
        total_sums[it] = sums[it] + jnp.sum(near_sums[it], axis=0)

        def send_total(k):
            remote(total_sums.at[it], far_sums.at[it, k - 1], sc_send.at[it, 1], sc_recv.at[it, 1], *far(k)).start()

        each(1, n_x * n_y, send_total)
        drain(arrived, ag_recv.at[it])
        if it + 1 < ITERS:
            gather(it + 1)
        drain(far_sums.at[it], sc_recv.at[it, 1])
        total = jnp.sum(total_sums[it] + jnp.sum(far_sums[it], axis=0), axis=1, keepdims=True)
        step = (total[0:1] - total[1:2]) / (total[0:1] + total[2:3])
        steps.append(step)
        fields.append([step * d for d in pieces])
        if it + 1 < ITERS:
            direc_lo[my_x, :, pl.ds(my_col, LANE)] = lo.astype(BF16)

            def send_lo(k, peer):
                piece = direc_lo.at[my_x, :, pl.ds(my_col, LANE)]
                remote(piece, piece, lo_send, lo_recv, band, peer).start()

            to_members(send_lo)

    drain(arrived, lo_recv)
    for r in range(lat // 8):
        first = direc[0, r].astype(F32) + direc_lo[r].astype(F32)
        moved = steps[0] * first + steps[1] * direc[1, r].astype(F32)
        for level in range(levels):
            out_ref[level, r * 8 : r * 8 + 8, :] = moved[level * 8 : level * 8 + 8]

    drain(got_obs, obs_send.at[0])
    drain(got_obs, obs_send.at[1])
    for it in range(ITERS):
        for level in range(last):
            drain(from_x.at[it, level], x_send.at[it, level])
            drain(from_z.at[it, level], z_send.at[it, level])
        drain(arrived.at[it], rs_send.at[it])
        drain(arrived, ag_send.at[it])
        drain(near_sums.at[it], sc_send.at[it, 0])
        drain(far_sums.at[it], sc_send.at[it, 1])
    drain(arrived, lo_send)


def local(n_band, n_member, ensemble, variance, obs_index, obs_value, obs_error, root_ranks):
    members_here, levels, lat, lon = ensemble.shape
    wide, mid, rows = lat + 2 * HALO, lat + 2 * HALF, levels * lat
    halves = members_here // QUAD
    rest = n_member - 1
    dma = pltpu.SemaphoreType.DMA
    vmem = pl.BlockSpec(memory_space=pltpu.VMEM)
    hbm = pl.BlockSpec(memory_space=pltpu.HBM)
    return pl.pallas_call(
        functools.partial(kernel, n_band, n_member, members_here, levels, lat, lon),
        out_shape=jax.ShapeDtypeStruct((levels, lat, lon), F32),
        in_specs=[hbm] * 6,
        out_specs=vmem,
        scratch_shapes=[
            pltpu.SMEM((ITERS,), jnp.int32),
            pltpu.VMEM((1, n_member * LANE), jnp.int32),
            pltpu.VMEM((1, n_member * LANE), F32),
            pltpu.VMEM((1, n_member * LANE), F32),
            pltpu.VMEM((members_here, levels, wide, lon), BF16),
            pltpu.VMEM((2 * BLK, BLK), BF16),
            pltpu.VMEM((QUAD * mid, QUAD * wide), BF16),
            pltpu.VMEM((QUAD * lat, QUAD * mid), BF16),
            pltpu.VMEM((n_member, 8, LANE), F32),
            pltpu.VMEM((rest, 8, LANE), F32),
            pltpu.VMEM((n_member, 8, LANE), F32),
            pltpu.VMEM((lon, n_member * LANE), BF16),
            pltpu.VMEM((2 * rows, n_member * LANE), BF16),
            pltpu.VMEM((2 * 8 * levels, n_member * LANE), BF16),
            pltpu.VMEM((1, n_member * LANE), F32),
            pltpu.VMEM((2 * 8 * levels, LANE), F32),
            pltpu.VMEM((ITERS, levels, wide, lon), F32),
            pltpu.VMEM((members_here * lat, lon + 2 * LANE), BF16),
            pltpu.VMEM((levels, members_here, wide, lon), BF16),
            pltpu.VMEM((halves, QUAD * mid, lon + 2 * LANE), BF16),
            pltpu.VMEM((halves, QUAD * mid, lon), BF16),
            pltpu.VMEM((ITERS, levels, lat, lon), F32),
            pltpu.VMEM((ITERS, levels - 1, lat // 8 - 1, 8, lon), F32),
            pltpu.VMEM((ITERS, levels - 1, 8, lon), F32),
            pltpu.VMEM((ITERS, levels - 1, lon // LANE - 1, 8, LANE), F32),
            pltpu.VMEM((ITERS, rest, 8, LANE), F32),
            pltpu.VMEM((levels, 8, LANE), F32),
            pltpu.VMEM((ITERS, lat // 8, 8 * levels, lon), BF16),
            pltpu.VMEM((lat // 8, 8 * levels, lon), BF16),
            pltpu.VMEM((ITERS, 8, LANE), F32),
            pltpu.VMEM((ITERS, 2 * (lon // LANE) - 1, 8, LANE), F32),
            pltpu.VMEM((ITERS, 8, LANE), F32),
            pltpu.VMEM((ITERS, (lat // 8) * (n_band // 2) - 1, 8, LANE), F32),
            dma((6,)),
            dma((2,)), dma((2,)),
            dma((2,)), dma((2,)),
            dma((ITERS, 2, lon // BLK)), dma((ITERS, 2, lon // BLK)),
            dma((ITERS, levels - 1)), dma((ITERS, levels - 1)),
            dma((ITERS, levels - 1)), dma((ITERS, levels - 1)),
            dma((ITERS,)), dma((ITERS,)),
            dma((ITERS,)), dma((ITERS,)),
            dma, dma,
            dma((ITERS, 2)), dma((ITERS, 2)),
        ],
        compiler_params=pltpu.CompilerParams(
            collective_id=0, has_side_effects=True, vmem_limit_bytes=65500 * 1024
        ),
    )(root_ranks, ensemble, variance, obs_index, obs_value, obs_error)


def solution(mesh):
    in_specs = (
        P("member", None, "band", None),
        P(None, "band", None),
        P("member", "band"),
        P("member", "band"),
        P("member", "band"),
        P(),
    )
    body = functools.partial(local, mesh.shape["band"], mesh.shape["member"])
    return jax.shard_map(body, mesh=mesh, in_specs=in_specs, out_specs=P(None, "band", None), check_vma=False)
```

```python
import functools
import math

import jax
import jax.numpy as jnp
from jax import lax
from jax.experimental import pallas as pl
from jax.experimental.pallas import tpu as pltpu
from jax.sharding import PartitionSpec as P

HALF = 8
ITERS = 2
LANE = 128
HALO = 2 * HALF
BLK = 256
QUAD = 4
GROUP = 4

huber_edge = 1.5
ensemble_share = 0.75
static_share = 0.25

F32 = jnp.float32
BF16 = jnp.bfloat16


def taps(distance, keep):
    raw = [math.exp(-0.5 * (k / (0.5 * HALF)) ** 2) for k in range(-HALF, HALF + 1)]
    norm = math.sqrt(sum(r * r for r in raw))
    scaled = distance.astype(F32) / (0.5 * HALF)
    entry = jnp.exp(-0.5 * scaled * scaled) / norm
    keep = keep & (jnp.abs(distance) <= HALF)
    return jnp.where(keep, entry, 0.0).astype(BF16)


def iota(shape, dim):
    return lax.broadcasted_iota(jnp.int32, shape, dim)


def split(x):
    hi = x.astype(BF16).astype(F32)
    return hi, x - hi


def kernel(
    n_band, n_member, members_here, levels, lat, lon,
    root_hbm, ens_ref, var_ref, idx_hbm, val_hbm, err_hbm, out_ref,
    root_ref, idx_ref, val_ref, err_ref,
    ext, wlon, lat1, lat2, send_obs, got_obs, obs, hot, lhs, lhs2, reached, grad2, gpad, edges, halo,
    xpad, ypad, zpad, vpad, spread, from_x, of_x, from_z, arrived, varp, direc, direc_lo,
    sums, near_sums, total_sums, far_sums,
    own_sem, ens_send, ens_recv, obs_send, obs_recv, group_recv, halo_send, halo_recv,
    x_send, x_recv, z_send, z_recv, rs_send, rs_recv, ag_send, ag_recv, lo_send, lo_recv, sc_send, sc_recv,
):
    me = lax.axis_index("member")
    band = lax.axis_index("band")
    rest = n_member - 1
    cols = lon // LANE
    wide = lat + 2 * HALO
    mid = lat + 2 * HALF
    rows = levels * lat
    up = lax.rem(band + 1, n_band)
    down = lax.rem(band + n_band - 1, n_band)
    my_x, my_z = me // cols, me % cols
    n_x, n_z, n_y = n_member // cols, cols, n_band // 2
    my_y, core = band // 2, band % 2
    my_row = pl.multiple_of(my_x * 8, 8)
    my_col = pl.multiple_of(my_z * LANE, LANE)
    last = levels - 1

    def remote(src, dst, send, recv, to_band, to_member):
        return pltpu.make_async_remote_copy(
            src_ref=src, dst_ref=dst, send_sem=send, recv_sem=recv,
            device_id=(to_band, to_member), device_id_type=pl.DeviceIdType.MESH,
        )

    def drain(ref, sem):
        pltpu.make_async_copy(ref, ref, sem).wait()

    def each(first, stop, start):
        def body(k, carry):
            start(k)
            return carry
        lax.fori_loop(first, stop, body, 0)

    def to_members(start):
        each(1, n_member, lambda k: start(k, lax.rem(me + k, n_member)))

    def near(k):
        index = lax.rem(core * n_z + my_z + k, 2 * n_z)
        return my_y * 2 + index // n_z, my_x * n_z + index % n_z

    def far(k):
        index = lax.rem(my_x * n_y + my_y + k, n_x * n_y)
        return (index % n_y) * 2 + core, (index // n_y) * n_z + my_z

    loads = [
        pltpu.make_async_copy(src, dst, own_sem.at[2 + i])
        for i, (src, dst) in enumerate(
            ((root_hbm, root_ref), (idx_hbm, idx_ref), (val_hbm, val_ref), (err_hbm, err_ref))
        )
    ]
    for load in loads:
        load.start()

    barrier = pltpu.get_barrier_semaphore()

    def greet(to_band, to_member):
        pl.semaphore_signal(
            barrier, inc=1, device_id=(to_band, to_member), device_id_type=pl.DeviceIdType.MESH
        )

    to_members(lambda k, peer: greet(band, peer))
    each(0, n_z, lambda k: greet(my_y * 2 + 1 - core, my_x * n_z + k))

    def greet_plane(k):
        greet(lax.rem(my_y + 1 + k // n_x, n_y) * 2 + core, (k % n_x) * n_z + my_z)

    greeted = n_x * (n_y - 1)
    each(0, greeted, greet_plane)
    greet(lax.rem(band + n_band + 2 * core - 1, n_band), me)
    greeted += n_member - 1 + n_z + 1

    own = pltpu.make_async_copy(ens_ref, ext.at[:, :, pl.ds(HALO, lat), :], own_sem.at[0])
    own.start()
    own_var = pltpu.make_async_copy(
        var_ref.at[:, pl.ds(my_row, 8), pl.ds(my_col, LANE)], varp, own_sem.at[1]
    )
    own_var.start()

    for load in loads:
        load.wait()

    flags = [(root_ref[it] == me).astype(F32) for it in range(ITERS)]
    for j in range(n_member):
        at = pl.ds(j * LANE, LANE)
        parts = [idx_ref[0:1, at].astype(F32), val_ref[0:1, at], err_ref[0:1, at]]
        lines = [part * flags[it] for it in range(ITERS) for part in parts]
        send_obs[j] = jnp.concatenate(lines + [jnp.zeros((2, LANE), F32)], axis=0)

    pl.semaphore_wait(barrier, greeted)

    to_members(
        lambda k, peer: remote(
            send_obs.at[peer], got_obs.at[k - 1], obs_send.at[0], obs_recv.at[0], band, peer
        ).start()
    )
    ens_up = remote(
        ens_ref.at[:, :, pl.ds(lat - HALO, HALO), :], ext.at[:, :, pl.ds(0, HALO), :],
        ens_send.at[0], ens_recv.at[0], up, me,
    )
    ens_down = remote(
        ens_ref.at[:, :, pl.ds(0, HALO), :], ext.at[:, :, pl.ds(HALO + lat, HALO), :],
        ens_send.at[1], ens_recv.at[1], down, me,
    )
    ens_up.start()
    ens_down.start()

    shape = (2 * BLK, BLK)
    wlon[...] = taps(iota(shape, 1) - iota(shape, 0) + LANE, iota(shape, 0) >= 0)
    shape = (QUAD * mid, QUAD * wide)
    target, source = iota(shape, 0), iota(shape, 1)
    row_out = band * lat - HALF + target % mid
    row_in = band * lat - HALO + source % wide
    all_rows = n_band * lat
    lat1[...] = taps(
        row_in - row_out,
        (target // mid == source // wide)
        & (row_out >= 0) & (row_out < all_rows) & (row_in >= 0) & (row_in < all_rows),
    )
    shape = (QUAD * lat, QUAD * mid)
    target, source = iota(shape, 0), iota(shape, 1)
    lat2[...] = taps(source % mid - HALF - target % lat, target // lat == source // mid)

    drain(got_obs, obs_recv.at[0])
    obs[me] = send_obs[me] + jnp.sum(got_obs[...], axis=0)
    to_members(
        lambda k, peer: remote(
            obs.at[me], obs.at[me], obs_send.at[1], group_recv.at[me // GROUP], band, peer
        ).start()
    )

    groups = n_member // GROUP
    width = GROUP * LANE

    def line(g, which):
        return jnp.concatenate([obs[g * GROUP + j, which : which + 1, :] for j in range(GROUP)], axis=1)

    def columns(g):
        return pl.ds(pl.multiple_of(g * width, width), width)

    def each_group(step):
        def body(g, carry):
            step(g)
            return carry
        lax.fori_loop(0, groups, body, 0)

    def hot_of(it, g):
        column = line(g, 3 * it).astype(jnp.int32) % lon
        for r in range(0, lon, LANE):
            hit = iota((LANE, width), 0) + r == column
            hot[r : r + LANE, columns(g)] = jnp.where(hit, 1.0, 0.0).astype(BF16)

    nt = (((1,), (1,)), ((), ()))

    def gather(it):
        field = direc[it - 1].reshape(rows, lon)

        def step(g):
            row = line(g, 3 * it).astype(jnp.int32) // lon
            level, in_level = row // lat, row % lat
            line_of = (in_level // 8) * (8 * levels) + level * 8 + in_level % 8
            found = jnp.dot(field, hot[:, columns(g)], preferred_element_type=F32)
            found = jnp.where(iota((rows, width), 0) == line_of, found, 0.0)
            reached[:, columns(g)] = jnp.sum(found, axis=0, keepdims=True)
        each_group(step)

    def terms_of(it, scale, g):
        values = line(g, 3 * it + 1)
        errors = line(g, 3 * it + 2)
        row = line(g, 3 * it).astype(jnp.int32) // lon
        departure = values
        if it > 0:
            departure = values - scale * reached[:, columns(g)]
        weight = huber_edge / jnp.maximum(jnp.abs(departure / errors), huber_edge)
        square = errors * errors
        hit = iota((rows, width), 0) == row
        for i, part in enumerate(split(weight * departure / square)):
            lhs[i * rows : (i + 1) * rows, columns(g)] = jnp.where(hit, part, 0.0).astype(BF16)
        mine = iota((8 * levels, width), 0)
        hit = (mine // 8) * lat + my_row + mine % 8 == row
        for i, part in enumerate(split(weight / square)):
            a = i * 8 * levels
            lhs2[a : a + 8 * levels, columns(g)] = jnp.where(hit, part, 0.0).astype(BF16)

    def halos(it, b):
        at = pl.ds(b * BLK, BLK)
        return [
            remote(
                edges.at[it, :, pl.ds((1 - side) * (lat - HALO), HALO), at], halo.at[it, side, :, :, at],
                halo_send.at[it, side, b], halo_recv.at[it, side, b], to, me,
            )
            for side, to in enumerate((up, down))
        ]

    def scatter(it):
        for b in range(lon // BLK):
            at = slice(b * BLK, (b + 1) * BLK)
            both = lax.dot_general(lhs[...], hot[at, :], nt, preferred_element_type=F32)
            block = both[:rows] + both[rows:]
            edges[it, :, :, at] = block.reshape(levels, lat, BLK).astype(BF16)
            gpad[it, :, :, at] = block.reshape(levels, lat, BLK)
            for copy in halos(it, b):
                copy.start()
        grad2[...] = lax.dot_general(
            lhs2[...], hot[pl.ds(my_col, LANE), :], nt, preferred_element_type=F32
        )

    def lon_filter(padded, store):
        for c in range(0, lon, BLK):
            at = slice(c, c + BLK)
            store(at, jnp.dot(padded[:, c : c + 2 * BLK], wlon[...], preferred_element_type=F32).astype(BF16))

    def put_padded(ref, at, block):
        ref[:, LANE + at.start : LANE + at.stop] = block
        if at.start == 0:
            ref[:, LANE + lon :] = block[:, :LANE]
        if at.stop == lon:
            ref[:, :LANE] = block[:, block.shape[1] - LANE :]

    def lon_of_rows(it, level, at_rows, gradients):
        for c in range(0, lon, BLK):
            at = slice(c, c + BLK)
            blocks = []
            for part, gradient in zip(at_rows, gradients):
                mixed = ext[:, level, part, at].astype(F32) * gradient[:, at].astype(F32)[None]
                blocks.append(mixed.astype(BF16).reshape(members_here * (part.stop - part.start), BLK))
            put_padded(xpad, at, jnp.concatenate(blocks, axis=0))

        def store(at, block):
            a = 0
            for part in at_rows:
                length = part.stop - part.start
                size = members_here * length
                ypad[level, :, part, at] = block[a : a + size].reshape(members_here, length, BLK)
                a += size

        lon_filter(xpad, store)

    def filters(it, level):
        lon_of_rows(
            it, level, (slice(0, HALO), slice(HALO + lat, wide)), (halo.at[it, 0, level], halo.at[it, 1, level])
        )
        for h in range(members_here // QUAD):
            who = slice(h * QUAD, (h + 1) * QUAD)
            zs, vs = zpad.at[h], vpad.at[h]
            for c in range(0, lon, BLK):
                at = slice(c, c + BLK)
                first = ypad[level, who, :, at].reshape(QUAD * wide, BLK)
                put_padded(zs, at, jnp.dot(lat1[...], first, preferred_element_type=F32).astype(BF16))

            def store_v(at, block):
                vs[:, at] = block

            lon_filter(zs, store_v)
            for c in range(0, lon, BLK):
                at = slice(c, c + BLK)
                second = jnp.dot(lat2[...], vs[:, at], preferred_element_type=F32).reshape(QUAD, lat, BLK)
                part = jnp.sum(ext[who, level, HALO : HALO + lat, at].astype(F32) * second, axis=0)
                if h == 0:
                    spread[it, level, :, at] = part
                else:
                    spread[it, level, :, at] += part

    steps = []
    fields = []
    my_group = me // GROUP
    for g, size in ((0, GROUP - 1), (None, GROUP)):
        def arrive(k):
            at = lax.rem(my_group + k, groups)
            drain(got_obs.at[pl.ds(0, size)], group_recv.at[at])
            hot_of(0, at)
            terms_of(0, None, at)

        if g == 0:
            arrive(0)
        else:
            each(1, groups, arrive)
    for it in range(ITERS):
        if it > 0:
            each_group(functools.partial(terms_of, it, steps[-1]))
        scatter(it)
        if it == 0:
            own.wait()
            own_var.wait()

        def middle(level, carry):
            lon_of_rows(it, level, (slice(HALO, HALO + lat),), (gpad.at[it, level],))
            return carry

        lax.fori_loop(0, levels, middle, 0)
        if it == 0:
            ens_up.wait()
            ens_down.wait()
        for b in range(lon // BLK):
            for copy in halos(it, b):
                copy.wait()

        def level_body(level, carry):
            filters(it, level)

            @pl.when(level < last)
            def _():
                def send_x(k):
                    to_x = lax.rem(my_x + k, n_x)
                    row = pl.multiple_of(to_x * 8, 8)
                    remote(
                        spread.at[it, level, pl.ds(row, 8), :], from_x.at[it, level, k - 1],
                        x_send.at[it, level], x_recv.at[it, level], band, to_x * n_z + my_z,
                    ).start()

                each(1, n_x, send_x)

            @pl.when(level == last)
            def _():
                def send(k, peer):
                    row = pl.multiple_of((peer // n_z) * 8, 8)
                    col = pl.multiple_of((peer % n_z) * LANE, LANE)
                    remote(
                        spread.at[it, last, pl.ds(row, 8), pl.ds(col, LANE)], arrived.at[it, k - 1],
                        rs_send.at[it], rs_recv.at[it], band, peer,
                    ).start()

                to_members(send)
            return carry

        lax.fori_loop(0, levels, level_body, 0)

        def pass_on(level):
            drain(from_x.at[it, level], x_recv.at[it, level])
            of_x[it, level] = spread[it, level, pl.ds(my_row, 8), :] + jnp.sum(from_x[it, level], axis=0)

            def send_z(k):
                to_z = lax.rem(my_z + k, n_z)
                col = pl.multiple_of(to_z * LANE, LANE)
                remote(
                    of_x.at[it, level, :, pl.ds(col, LANE)], from_z.at[it, level, k - 1],
                    z_send.at[it, level], z_recv.at[it, level], band, my_x * n_z + to_z,
                ).start()

            each(1, n_z, send_z)

        each(0, last, pass_on)

        along = jnp.zeros((8, LANE), F32)
        back = jnp.zeros((8, LANE), F32)
        curve = jnp.zeros((8, LANE), F32)
        pieces = []
        for level in range(levels):
            if level < last:
                drain(from_z.at[it, level], z_recv.at[it, level])
                summed = of_x[it, level, :, pl.ds(my_col, LANE)] + jnp.sum(from_z[it, level], axis=0)
            else:
                drain(arrived.at[it], rs_recv.at[it])
                summed = spread[it, level, pl.ds(my_row, 8), pl.ds(my_col, LANE)] + jnp.sum(arrived[it], axis=0)
            g = gpad[it, level, pl.ds(my_row, 8), pl.ds(my_col, LANE)]
            d = ensemble_share * summed / (members_here * n_member - 1) + static_share * varp[level] * g
            a = level * 8
            c = grad2[a : a + 8, :] + grad2[a + 8 * levels : a + 8 * levels + 8, :]
            along += g * d
            curve += c * d * d
            if it > 0:
                back += fields[-1][level] * g
            pieces.append(d)
        sums[it] = jnp.concatenate(
            [jnp.sum(x, axis=0, keepdims=True) for x in (along, back, curve)] + [jnp.zeros((5, LANE), F32)], axis=0
        )

        def send_sums(k):
            remote(sums.at[it], near_sums.at[it, k - 1], sc_send.at[it, 0], sc_recv.at[it, 0], *near(k)).start()

        each(1, 2 * n_z, send_sums)
        hi, lo = split(jnp.concatenate(pieces, axis=0))
        direc[it, my_x, :, pl.ds(my_col, LANE)] = hi.astype(BF16)

        def send_piece(k, peer):
            piece = direc.at[it, my_x, :, pl.ds(my_col, LANE)]
            remote(piece, piece, ag_send.at[it], ag_recv.at[it], band, peer).start()

        to_members(send_piece)
        if it + 1 < ITERS:
            each_group(functools.partial(hot_of, it + 1))
        drain(near_sums.at[it], sc_recv.at[it, 0])
        total_sums[it] = sums[it] + jnp.sum(near_sums[it], axis=0)

        def send_total(k):
            remote(total_sums.at[it], far_sums.at[it, k - 1], sc_send.at[it, 1], sc_recv.at[it, 1], *far(k)).start()

        each(1, n_x * n_y, send_total)
        drain(arrived, ag_recv.at[it])
        if it + 1 < ITERS:
            gather(it + 1)
        drain(far_sums.at[it], sc_recv.at[it, 1])
        total = jnp.sum(total_sums[it] + jnp.sum(far_sums[it], axis=0), axis=1, keepdims=True)
        step = (total[0:1] - total[1:2]) / (total[0:1] + total[2:3])
        steps.append(step)
        fields.append([step * d for d in pieces])
        if it + 1 < ITERS:
            direc_lo[my_x, :, pl.ds(my_col, LANE)] = lo.astype(BF16)

            def send_lo(k, peer):
                piece = direc_lo.at[my_x, :, pl.ds(my_col, LANE)]
                remote(piece, piece, lo_send, lo_recv, band, peer).start()

            to_members(send_lo)

    drain(arrived, lo_recv)
    for r in range(lat // 8):
        first = direc[0, r].astype(F32) + direc_lo[r].astype(F32)
        moved = steps[0] * first + steps[1] * direc[1, r].astype(F32)
        for level in range(levels):
            out_ref[level, r * 8 : r * 8 + 8, :] = moved[level * 8 : level * 8 + 8]

    drain(got_obs, obs_send.at[0])
    drain(got_obs, obs_send.at[1])
    for it in range(ITERS):
        for level in range(last):
            drain(from_x.at[it, level], x_send.at[it, level])
            drain(from_z.at[it, level], z_send.at[it, level])
        drain(arrived.at[it], rs_send.at[it])
        drain(arrived, ag_send.at[it])
        drain(near_sums.at[it], sc_send.at[it, 0])
        drain(far_sums.at[it], sc_send.at[it, 1])
    drain(arrived, lo_send)


def local(n_band, n_member, ensemble, variance, obs_index, obs_value, obs_error, root_ranks):
    members_here, levels, lat, lon = ensemble.shape
    wide, mid, rows = lat + 2 * HALO, lat + 2 * HALF, levels * lat
    halves = members_here // QUAD
    rest = n_member - 1
    dma = pltpu.SemaphoreType.DMA
    vmem = pl.BlockSpec(memory_space=pltpu.VMEM)
    hbm = pl.BlockSpec(memory_space=pltpu.HBM)
    return pl.pallas_call(
        functools.partial(kernel, n_band, n_member, members_here, levels, lat, lon),
        out_shape=jax.ShapeDtypeStruct((levels, lat, lon), F32),
        in_specs=[hbm] * 6,
        out_specs=vmem,
        scratch_shapes=[
            pltpu.SMEM((ITERS,), jnp.int32),
            pltpu.VMEM((1, n_member * LANE), jnp.int32),
            pltpu.VMEM((1, n_member * LANE), F32),
            pltpu.VMEM((1, n_member * LANE), F32),
            pltpu.VMEM((members_here, levels, wide, lon), BF16),
            pltpu.VMEM((2 * BLK, BLK), BF16),
            pltpu.VMEM((QUAD * mid, QUAD * wide), BF16),
            pltpu.VMEM((QUAD * lat, QUAD * mid), BF16),
            pltpu.VMEM((n_member, 8, LANE), F32),
            pltpu.VMEM((rest, 8, LANE), F32),
            pltpu.VMEM((n_member, 8, LANE), F32),
            pltpu.VMEM((lon, n_member * LANE), BF16),
            pltpu.VMEM((2 * rows, n_member * LANE), BF16),
            pltpu.VMEM((2 * 8 * levels, n_member * LANE), BF16),
            pltpu.VMEM((1, n_member * LANE), F32),
            pltpu.VMEM((2 * 8 * levels, LANE), F32),
            pltpu.VMEM((ITERS, levels, lat, lon), F32),
            pltpu.VMEM((ITERS, levels, lat, lon), BF16),
            pltpu.VMEM((ITERS, 2, levels, HALO, lon), BF16),
            pltpu.VMEM((members_here * lat, lon + 2 * LANE), BF16),
            pltpu.VMEM((levels, members_here, wide, lon), BF16),
            pltpu.VMEM((halves, QUAD * mid, lon + 2 * LANE), BF16),
            pltpu.VMEM((halves, QUAD * mid, lon), BF16),
            pltpu.VMEM((ITERS, levels, lat, lon), F32),
            pltpu.VMEM((ITERS, levels - 1, lat // 8 - 1, 8, lon), F32),
            pltpu.VMEM((ITERS, levels - 1, 8, lon), F32),
            pltpu.VMEM((ITERS, levels - 1, lon // LANE - 1, 8, LANE), F32),
            pltpu.VMEM((ITERS, rest, 8, LANE), F32),
            pltpu.VMEM((levels, 8, LANE), F32),
            pltpu.VMEM((ITERS, lat // 8, 8 * levels, lon), BF16),
            pltpu.VMEM((lat // 8, 8 * levels, lon), BF16),
            pltpu.VMEM((ITERS, 8, LANE), F32),
            pltpu.VMEM((ITERS, 2 * (lon // LANE) - 1, 8, LANE), F32),
            pltpu.VMEM((ITERS, 8, LANE), F32),
            pltpu.VMEM((ITERS, (lat // 8) * (n_band // 2) - 1, 8, LANE), F32),
            dma((6,)),
            dma((2,)), dma((2,)),
            dma((2,)), dma((1,)), dma((n_member // GROUP,)),
            dma((ITERS, 2, lon // BLK)), dma((ITERS, 2, lon // BLK)),
            dma((ITERS, levels - 1)), dma((ITERS, levels - 1)),
            dma((ITERS, levels - 1)), dma((ITERS, levels - 1)),
            dma((ITERS,)), dma((ITERS,)),
            dma((ITERS,)), dma((ITERS,)),
            dma, dma,
            dma((ITERS, 2)), dma((ITERS, 2)),
        ],
        compiler_params=pltpu.CompilerParams(
            collective_id=0, has_side_effects=True, vmem_limit_bytes=65500 * 1024
        ),
    )(root_ranks, ensemble, variance, obs_index, obs_value, obs_error)


def solution(mesh):
    in_specs = (
        P("member", None, "band", None),
        P(None, "band", None),
        P("member", "band"),
        P("member", "band"),
        P("member", "band"),
        P(),
    )
    body = functools.partial(local, mesh.shape["band"], mesh.shape["member"])
    return jax.shard_map(body, mesh=mesh, in_specs=in_specs, out_specs=P(None, "band", None), check_vma=False)
```

```python
import functools
import math

import jax
import jax.numpy as jnp
from jax import lax
from jax.experimental import pallas as pl
from jax.experimental.pallas import tpu as pltpu
from jax.sharding import PartitionSpec as P

HALF = 8
ITERS = 2
LANE = 128
HALO = 2 * HALF
BLK = 256
QUAD = 4
GROUP = 4

huber_edge = 1.5
ensemble_share = 0.75
static_share = 0.25

F32 = jnp.float32
BF16 = jnp.bfloat16


def taps(distance, keep):
    raw = [math.exp(-0.5 * (k / (0.5 * HALF)) ** 2) for k in range(-HALF, HALF + 1)]
    norm = math.sqrt(sum(r * r for r in raw))
    scaled = distance.astype(F32) / (0.5 * HALF)
    entry = jnp.exp(-0.5 * scaled * scaled) / norm
    keep = keep & (jnp.abs(distance) <= HALF)
    return jnp.where(keep, entry, 0.0).astype(BF16)


def iota(shape, dim):
    return lax.broadcasted_iota(jnp.int32, shape, dim)


def split(x):
    hi = x.astype(BF16).astype(F32)
    return hi, x - hi


def kernel(
    n_band, n_member, members_here, levels, lat, lon,
    root_hbm, ens_ref, var_ref, idx_hbm, val_hbm, err_hbm, out_ref,
    root_ref, idx_ref, val_ref, err_ref,
    ext, wlon, lat1, lat2, send_obs, got_obs, obs, hot, lhs, lhs2, reached, grad2, gpad, edges, halo,
    xpad, ypad, zpad, vpad, spread, from_x, of_x, from_z, arrived, varp, direc, direc_lo,
    sums, near_sums, total_sums, far_sums,
    own_sem, ens_send, ens_recv, obs_send, obs_recv, group_recv, halo_send, halo_recv,
    x_send, x_recv, z_send, z_recv, rs_send, rs_recv, ag_send, ag_recv, lo_send, lo_recv, sc_send, sc_recv,
):
    me = lax.axis_index("member")
    band = lax.axis_index("band")
    rest = n_member - 1
    cols = lon // LANE
    wide = lat + 2 * HALO
    mid = lat + 2 * HALF
    rows = levels * lat
    up = lax.rem(band + 1, n_band)
    down = lax.rem(band + n_band - 1, n_band)
    my_x, my_z = me // cols, me % cols
    n_x, n_z, n_y = n_member // cols, cols, n_band // 2
    my_y, core = band // 2, band % 2
    my_row = pl.multiple_of(my_x * 8, 8)
    my_col = pl.multiple_of(my_z * LANE, LANE)
    last = levels - 1

    def remote(src, dst, send, recv, to_band, to_member):
        return pltpu.make_async_remote_copy(
            src_ref=src, dst_ref=dst, send_sem=send, recv_sem=recv,
            device_id=(to_band, to_member), device_id_type=pl.DeviceIdType.MESH,
        )

    def drain(ref, sem):
        pltpu.make_async_copy(ref, ref, sem).wait()

    def each(first, stop, start):
        def body(k, carry):
            start(k)
            return carry
        lax.fori_loop(first, stop, body, 0)

    def to_members(start):
        each(1, n_member, lambda k: start(k, lax.rem(me + k, n_member)))

    def near(k):
        index = lax.rem(core * n_z + my_z + k, 2 * n_z)
        return my_y * 2 + index // n_z, my_x * n_z + index % n_z

    def far(k):
        index = lax.rem(my_x * n_y + my_y + k, n_x * n_y)
        return (index % n_y) * 2 + core, (index // n_y) * n_z + my_z

    loads = [
        pltpu.make_async_copy(src, dst, own_sem.at[2 + i])
        for i, (src, dst) in enumerate(
            ((root_hbm, root_ref), (idx_hbm, idx_ref), (val_hbm, val_ref), (err_hbm, err_ref))
        )
    ]
    for load in loads:
        load.start()

    barrier = pltpu.get_barrier_semaphore()

    def greet(to_band, to_member):
        pl.semaphore_signal(
            barrier, inc=1, device_id=(to_band, to_member), device_id_type=pl.DeviceIdType.MESH
        )

    to_members(lambda k, peer: greet(band, peer))
    each(0, n_z, lambda k: greet(my_y * 2 + 1 - core, my_x * n_z + k))

    def greet_plane(k):
        greet(lax.rem(my_y + 1 + k // n_x, n_y) * 2 + core, (k % n_x) * n_z + my_z)

    greeted = n_x * (n_y - 1)
    each(0, greeted, greet_plane)
    greet(lax.rem(band + n_band + 2 * core - 1, n_band), me)
    greeted += n_member - 1 + n_z + 1

    own = pltpu.make_async_copy(ens_ref, ext.at[:, :, pl.ds(HALO, lat), :], own_sem.at[0])
    own.start()
    own_var = pltpu.make_async_copy(
        var_ref.at[:, pl.ds(my_row, 8), pl.ds(my_col, LANE)], varp, own_sem.at[1]
    )
    own_var.start()

    for load in loads:
        load.wait()

    flags = [(root_ref[it] == me).astype(F32) for it in range(ITERS)]
    for j in range(n_member):
        at = pl.ds(j * LANE, LANE)
        parts = [idx_ref[0:1, at].astype(F32), val_ref[0:1, at], err_ref[0:1, at]]
        lines = [part * flags[it] for it in range(ITERS) for part in parts]
        send_obs[j] = jnp.concatenate(lines + [jnp.zeros((2, LANE), F32)], axis=0)

    pl.semaphore_wait(barrier, greeted)

    to_members(
        lambda k, peer: remote(
            send_obs.at[peer], got_obs.at[k - 1], obs_send.at[0], obs_recv.at[0], band, peer
        ).start()
    )
    ens_up = remote(
        ens_ref.at[:, :, pl.ds(lat - HALO, HALO), :], ext.at[:, :, pl.ds(0, HALO), :],
        ens_send.at[0], ens_recv.at[0], up, me,
    )
    ens_down = remote(
        ens_ref.at[:, :, pl.ds(0, HALO), :], ext.at[:, :, pl.ds(HALO + lat, HALO), :],
        ens_send.at[1], ens_recv.at[1], down, me,
    )
    ens_up.start()
    ens_down.start()

    shape = (2 * BLK, BLK)
    wlon[...] = taps(iota(shape, 1) - iota(shape, 0) + LANE, iota(shape, 0) >= 0)
    shape = (QUAD * mid, QUAD * wide)
    target, source = iota(shape, 0), iota(shape, 1)
    row_out = band * lat - HALF + target % mid
    row_in = band * lat - HALO + source % wide
    all_rows = n_band * lat
    lat1[...] = taps(
        row_in - row_out,
        (target // mid == source // wide)
        & (row_out >= 0) & (row_out < all_rows) & (row_in >= 0) & (row_in < all_rows),
    )
    shape = (QUAD * lat, QUAD * mid)
    target, source = iota(shape, 0), iota(shape, 1)
    lat2[...] = taps(source % mid - HALF - target % lat, target // lat == source // mid)

    drain(got_obs, obs_recv.at[0])
    obs[me] = send_obs[me] + jnp.sum(got_obs[...], axis=0)
    to_members(
        lambda k, peer: remote(
            obs.at[me], obs.at[me], obs_send.at[1], group_recv.at[me // GROUP], band, peer
        ).start()
    )

    groups = n_member // GROUP
    width = GROUP * LANE

    def line(g, which):
        return jnp.concatenate([obs[g * GROUP + j, which : which + 1, :] for j in range(GROUP)], axis=1)

    def columns(g):
        return pl.ds(pl.multiple_of(g * width, width), width)

    def each_group(step):
        def body(g, carry):
            step(g)
            return carry
        lax.fori_loop(0, groups, body, 0)

    def hot_of(it, g):
        column = line(g, 3 * it).astype(jnp.int32) % lon
        for r in range(0, lon, LANE):
            hit = iota((LANE, width), 0) + r == column
            hot[r : r + LANE, columns(g)] = jnp.where(hit, 1.0, 0.0).astype(BF16)

    nt = (((1,), (1,)), ((), ()))

    def gather(it):
        field = direc[it - 1].reshape(rows, lon)

        def step(g):
            row = line(g, 3 * it).astype(jnp.int32) // lon
            level, in_level = row // lat, row % lat
            line_of = (in_level // 8) * (8 * levels) + level * 8 + in_level % 8
            found = jnp.dot(field, hot[:, columns(g)], preferred_element_type=F32)
            found = jnp.where(iota((rows, width), 0) == line_of, found, 0.0)
            reached[:, columns(g)] = jnp.sum(found, axis=0, keepdims=True)
        each_group(step)

    def terms_of(it, scale, g):
        values = line(g, 3 * it + 1)
        errors = line(g, 3 * it + 2)
        row = line(g, 3 * it).astype(jnp.int32) // lon
        departure = values
        if it > 0:
            departure = values - scale * reached[:, columns(g)]
        weight = huber_edge / jnp.maximum(jnp.abs(departure / errors), huber_edge)
        square = errors * errors
        hit = iota((rows, width), 0) == row
        for i, part in enumerate(split(weight * departure / square)):
            lhs[i * rows : (i + 1) * rows, columns(g)] = jnp.where(hit, part, 0.0).astype(BF16)
        mine = iota((8 * levels, width), 0)
        hit = (mine // 8) * lat + my_row + mine % 8 == row
        for i, part in enumerate(split(weight / square)):
            a = i * 8 * levels
            lhs2[a : a + 8 * levels, columns(g)] = jnp.where(hit, part, 0.0).astype(BF16)

    def halos(it, b):
        at = pl.ds(b * BLK, BLK)
        return [
            remote(
                edges.at[it, :, pl.ds((1 - side) * (lat - HALO), HALO), at], halo.at[it, side, :, :, at],
                halo_send.at[it, side, b], halo_recv.at[it, side, b], to, me,
            )
            for side, to in enumerate((up, down))
        ]

    def scatter(it):
        for b in range(lon // BLK):
            at = slice(b * BLK, (b + 1) * BLK)
            both = lax.dot_general(lhs[...], hot[at, :], nt, preferred_element_type=F32)
            block = both[:rows] + both[rows:]
            edges[it, :, :, at] = block.reshape(levels, lat, BLK).astype(BF16)
            gpad[it, :, :, at] = block.reshape(levels, lat, BLK)
            for copy in halos(it, b):
                copy.start()
        grad2[...] = lax.dot_general(
            lhs2[...], hot[pl.ds(my_col, LANE), :], nt, preferred_element_type=F32
        )

    def lon_filter(padded, store):
        for c in range(0, lon, BLK):
            at = slice(c, c + BLK)
            store(at, jnp.dot(padded[:, c : c + 2 * BLK], wlon[...], preferred_element_type=F32).astype(BF16))

    def put_padded(ref, at, block):
        ref[:, LANE + at.start : LANE + at.stop] = block
        if at.start == 0:
            ref[:, LANE + lon :] = block[:, :LANE]
        if at.stop == lon:
            ref[:, :LANE] = block[:, block.shape[1] - LANE :]

    def lon_of_rows(it, level, at_rows, gradients):
        for c in range(0, lon, BLK):
            at = slice(c, c + BLK)
            blocks = []
            for part, gradient in zip(at_rows, gradients):
                mixed = ext[:, level, part, at].astype(F32) * gradient[:, at].astype(F32)[None]
                blocks.append(mixed.astype(BF16).reshape(members_here * (part.stop - part.start), BLK))
            put_padded(xpad, at, jnp.concatenate(blocks, axis=0))

        def store(at, block):
            a = 0
            for part in at_rows:
                length = part.stop - part.start
                size = members_here * length
                ypad[level, :, part, at] = block[a : a + size].reshape(members_here, length, BLK)
                a += size

        lon_filter(xpad, store)

    def filters(it, level):
        lon_of_rows(
            it, level, (slice(0, HALO), slice(HALO + lat, wide)), (halo.at[it, 0, level], halo.at[it, 1, level])
        )
        for h in range(members_here // QUAD):
            who = slice(h * QUAD, (h + 1) * QUAD)
            zs, vs = zpad.at[h], vpad.at[h]
            for c in range(0, lon, BLK):
                at = slice(c, c + BLK)
                first = ypad[level, who, :, at].reshape(QUAD * wide, BLK)
                put_padded(zs, at, jnp.dot(lat1[...], first, preferred_element_type=F32).astype(BF16))

            def store_v(at, block):
                vs[:, at] = block

            lon_filter(zs, store_v)
            for c in range(0, lon, BLK):
                at = slice(c, c + BLK)
                second = jnp.dot(lat2[...], vs[:, at], preferred_element_type=F32).reshape(QUAD, lat, BLK)
                part = jnp.sum(ext[who, level, HALO : HALO + lat, at].astype(F32) * second, axis=0)
                if h == 0:
                    spread[it, level, :, at] = part
                else:
                    spread[it, level, :, at] += part

    steps = []
    fields = []
    my_group = me // GROUP
    for g, size in ((0, GROUP - 1), (None, GROUP)):
        def arrive(k):
            at = lax.rem(my_group + k, groups)
            drain(got_obs.at[pl.ds(0, size)], group_recv.at[at])
            hot_of(0, at)
            terms_of(0, None, at)

        if g == 0:
            arrive(0)
        else:
            each(1, groups, arrive)
    for it in range(ITERS):
        if it > 0:
            each_group(functools.partial(terms_of, it, steps[-1]))
        scatter(it)
        if it == 0:
            own.wait()
            own_var.wait()

        def middle(level, carry):
            lon_of_rows(it, level, (slice(HALO, HALO + lat),), (gpad.at[it, level],))
            return carry

        lax.fori_loop(0, levels, middle, 0)
        if it == 0:
            ens_up.wait()
            ens_down.wait()
        for b in range(lon // BLK):
            for copy in halos(it, b):
                copy.wait()

        def level_body(level, carry):
            filters(it, level)

            @pl.when(level < last)
            def _():
                def send_x(k):
                    to_x = lax.rem(my_x + k, n_x)
                    row = pl.multiple_of(to_x * 8, 8)
                    remote(
                        spread.at[it, level, pl.ds(row, 8), :], from_x.at[it, level, k - 1],
                        x_send.at[it, level], x_recv.at[it, level], band, to_x * n_z + my_z,
                    ).start()

                each(1, n_x, send_x)

            @pl.when(level == last)
            def _():
                def send(k, peer):
                    row = pl.multiple_of((peer // n_z) * 8, 8)
                    col = pl.multiple_of((peer % n_z) * LANE, LANE)
                    remote(
                        spread.at[it, last, pl.ds(row, 8), pl.ds(col, LANE)], arrived.at[it, k - 1],
                        rs_send.at[it], rs_recv.at[it], band, peer,
                    ).start()

                to_members(send)
            return carry

        lax.fori_loop(0, levels, level_body, 0)

        def pass_on(level):
            drain(from_x.at[it, level], x_recv.at[it, level])
            of_x[it, level] = spread[it, level, pl.ds(my_row, 8), :] + jnp.sum(from_x[it, level], axis=0)

            def send_z(k):
                to_z = lax.rem(my_z + k, n_z)
                col = pl.multiple_of(to_z * LANE, LANE)
                remote(
                    of_x.at[it, level, :, pl.ds(col, LANE)], from_z.at[it, level, k - 1],
                    z_send.at[it, level], z_recv.at[it, level], band, my_x * n_z + to_z,
                ).start()

            each(1, n_z, send_z)

        each(0, last, pass_on)

        along = jnp.zeros((8, LANE), F32)
        back = jnp.zeros((8, LANE), F32)
        curve = jnp.zeros((8, LANE), F32)
        pieces = []
        for level in range(levels):
            if level < last:
                drain(from_z.at[it, level], z_recv.at[it, level])
                summed = of_x[it, level, :, pl.ds(my_col, LANE)] + jnp.sum(from_z[it, level], axis=0)
            else:
                drain(arrived.at[it], rs_recv.at[it])
                summed = spread[it, level, pl.ds(my_row, 8), pl.ds(my_col, LANE)] + jnp.sum(arrived[it], axis=0)
            g = gpad[it, level, pl.ds(my_row, 8), pl.ds(my_col, LANE)]
            d = ensemble_share * summed / (members_here * n_member - 1) + static_share * varp[level] * g
            a = level * 8
            c = grad2[a : a + 8, :] + grad2[a + 8 * levels : a + 8 * levels + 8, :]
            along += g * d
            curve += c * d * d
            if it > 0:
                back += fields[-1][level] * g
            pieces.append(d)
        sums[it] = jnp.concatenate(
            [jnp.sum(x, axis=0, keepdims=True) for x in (along, back, curve)] + [jnp.zeros((5, LANE), F32)], axis=0
        )

        def send_sums(k):
            remote(sums.at[it], near_sums.at[it, k - 1], sc_send.at[it, 0], sc_recv.at[it, 0], *near(k)).start()

        each(1, 2 * n_z, send_sums)
        hi, lo = split(jnp.concatenate(pieces, axis=0))
        direc[it, my_x, :, pl.ds(my_col, LANE)] = hi.astype(BF16)

        def send_piece(k, peer):
            piece = direc.at[it, my_x, :, pl.ds(my_col, LANE)]
            remote(piece, piece, ag_send.at[it], ag_recv.at[it], band, peer).start()

        to_members(send_piece)
        if it + 1 < ITERS:
            each_group(functools.partial(hot_of, it + 1))
        drain(near_sums.at[it], sc_recv.at[it, 0])
        total_sums[it] = sums[it] + jnp.sum(near_sums[it], axis=0)

        def send_total(k):
            remote(total_sums.at[it], far_sums.at[it, k - 1], sc_send.at[it, 1], sc_recv.at[it, 1], *far(k)).start()

        each(1, n_x * n_y, send_total)
        if it + 1 == ITERS:
            drain(arrived, lo_recv)
            for r in range(lat // 8):
                out_ref[r] = steps[0] * (direc[0, r].astype(F32) + direc_lo[r].astype(F32))
        drain(arrived, ag_recv.at[it])
        if it + 1 < ITERS:
            gather(it + 1)
        drain(far_sums.at[it], sc_recv.at[it, 1])
        total = jnp.sum(total_sums[it] + jnp.sum(far_sums[it], axis=0), axis=1, keepdims=True)
        step = (total[0:1] - total[1:2]) / (total[0:1] + total[2:3])
        steps.append(step)
        fields.append([step * d for d in pieces])
        if it + 1 < ITERS:
            direc_lo[my_x, :, pl.ds(my_col, LANE)] = lo.astype(BF16)

            def send_lo(k, peer):
                piece = direc_lo.at[my_x, :, pl.ds(my_col, LANE)]
                remote(piece, piece, lo_send, lo_recv, band, peer).start()

            to_members(send_lo)

    for r in range(lat // 8):
        out_ref[r] += steps[1] * direc[1, r].astype(F32)

    drain(got_obs, obs_send.at[0])
    drain(got_obs, obs_send.at[1])
    for it in range(ITERS):
        for level in range(last):
            drain(from_x.at[it, level], x_send.at[it, level])
            drain(from_z.at[it, level], z_send.at[it, level])
        drain(arrived.at[it], rs_send.at[it])
        drain(arrived, ag_send.at[it])
        drain(near_sums.at[it], sc_send.at[it, 0])
        drain(far_sums.at[it], sc_send.at[it, 1])
    drain(arrived, lo_send)


def local(n_band, n_member, ensemble, variance, obs_index, obs_value, obs_error, root_ranks):
    members_here, levels, lat, lon = ensemble.shape
    wide, mid, rows = lat + 2 * HALO, lat + 2 * HALF, levels * lat
    halves = members_here // QUAD
    rest = n_member - 1
    dma = pltpu.SemaphoreType.DMA
    vmem = pl.BlockSpec(memory_space=pltpu.VMEM)
    hbm = pl.BlockSpec(memory_space=pltpu.HBM)
    out = pl.pallas_call(
        functools.partial(kernel, n_band, n_member, members_here, levels, lat, lon),
        out_shape=jax.ShapeDtypeStruct((lat // 8, 8 * levels, lon), F32),
        in_specs=[hbm] * 6,
        out_specs=vmem,
        scratch_shapes=[
            pltpu.SMEM((ITERS,), jnp.int32),
            pltpu.VMEM((1, n_member * LANE), jnp.int32),
            pltpu.VMEM((1, n_member * LANE), F32),
            pltpu.VMEM((1, n_member * LANE), F32),
            pltpu.VMEM((members_here, levels, wide, lon), BF16),
            pltpu.VMEM((2 * BLK, BLK), BF16),
            pltpu.VMEM((QUAD * mid, QUAD * wide), BF16),
            pltpu.VMEM((QUAD * lat, QUAD * mid), BF16),
            pltpu.VMEM((n_member, 8, LANE), F32),
            pltpu.VMEM((rest, 8, LANE), F32),
            pltpu.VMEM((n_member, 8, LANE), F32),
            pltpu.VMEM((lon, n_member * LANE), BF16),
            pltpu.VMEM((2 * rows, n_member * LANE), BF16),
            pltpu.VMEM((2 * 8 * levels, n_member * LANE), BF16),
            pltpu.VMEM((1, n_member * LANE), F32),
            pltpu.VMEM((2 * 8 * levels, LANE), F32),
            pltpu.VMEM((ITERS, levels, lat, lon), F32),
            pltpu.VMEM((ITERS, levels, lat, lon), BF16),
            pltpu.VMEM((ITERS, 2, levels, HALO, lon), BF16),
            pltpu.VMEM((members_here * lat, lon + 2 * LANE), BF16),
            pltpu.VMEM((levels, members_here, wide, lon), BF16),
            pltpu.VMEM((halves, QUAD * mid, lon + 2 * LANE), BF16),
            pltpu.VMEM((halves, QUAD * mid, lon), BF16),
            pltpu.VMEM((ITERS, levels, lat, lon), F32),
            pltpu.VMEM((ITERS, levels - 1, lat // 8 - 1, 8, lon), F32),
            pltpu.VMEM((ITERS, levels - 1, 8, lon), F32),
            pltpu.VMEM((ITERS, levels - 1, lon // LANE - 1, 8, LANE), F32),
            pltpu.VMEM((ITERS, rest, 8, LANE), F32),
            pltpu.VMEM((levels, 8, LANE), F32),
            pltpu.VMEM((ITERS, lat // 8, 8 * levels, lon), BF16),
            pltpu.VMEM((lat // 8, 8 * levels, lon), BF16),
            pltpu.VMEM((ITERS, 8, LANE), F32),
            pltpu.VMEM((ITERS, 2 * (lon // LANE) - 1, 8, LANE), F32),
            pltpu.VMEM((ITERS, 8, LANE), F32),
            pltpu.VMEM((ITERS, (lat // 8) * (n_band // 2) - 1, 8, LANE), F32),
            dma((6,)),
            dma((2,)), dma((2,)),
            dma((2,)), dma((1,)), dma((n_member // GROUP,)),
            dma((ITERS, 2, lon // BLK)), dma((ITERS, 2, lon // BLK)),
            dma((ITERS, levels - 1)), dma((ITERS, levels - 1)),
            dma((ITERS, levels - 1)), dma((ITERS, levels - 1)),
            dma((ITERS,)), dma((ITERS,)),
            dma((ITERS,)), dma((ITERS,)),
            dma, dma,
            dma((ITERS, 2)), dma((ITERS, 2)),
        ],
        compiler_params=pltpu.CompilerParams(
            collective_id=0, has_side_effects=True, vmem_limit_bytes=65500 * 1024
        ),
    )(root_ranks, ensemble, variance, obs_index, obs_value, obs_error)
    return jnp.swapaxes(out.reshape(lat // 8, levels, 8, lon), 0, 1).reshape(levels, lat, lon)


def solution(mesh):
    in_specs = (
        P("member", None, "band", None),
        P(None, "band", None),
        P("member", "band"),
        P("member", "band"),
        P("member", "band"),
        P(),
    )
    body = functools.partial(local, mesh.shape["band"], mesh.shape["member"])
    return jax.shard_map(body, mesh=mesh, in_specs=in_specs, out_specs=P(None, "band", None), check_vma=False)
```

```python
import functools
import math

import jax
import jax.numpy as jnp
from jax import lax
from jax.experimental import pallas as pl
from jax.experimental.pallas import tpu as pltpu
from jax.sharding import PartitionSpec as P

HALF = 8
ITERS = 2
LANE = 128
HALO = 2 * HALF
BLK = 256
QUAD = 4
GROUP = 4

huber_edge = 1.5
ensemble_share = 0.75
static_share = 0.25

F32 = jnp.float32
BF16 = jnp.bfloat16


def taps(distance, keep):
    raw = [math.exp(-0.5 * (k / (0.5 * HALF)) ** 2) for k in range(-HALF, HALF + 1)]
    norm = math.sqrt(sum(r * r for r in raw))
    scaled = distance.astype(F32) / (0.5 * HALF)
    entry = jnp.exp(-0.5 * scaled * scaled) / norm
    keep = keep & (jnp.abs(distance) <= HALF)
    return jnp.where(keep, entry, 0.0).astype(BF16)


def iota(shape, dim):
    return lax.broadcasted_iota(jnp.int32, shape, dim)


def split(x):
    hi = x.astype(BF16).astype(F32)
    return hi, x - hi


def kernel(
    n_band, n_member, members_here, levels, lat, lon,
    root_hbm, ens_ref, var_ref, idx_hbm, val_hbm, err_hbm, out_ref,
    root_ref, idx_ref, val_ref, err_ref,
    ext, wlon, lat1, lat2, send_obs, got_obs, obs, hot, lhs, lhs2, reached, grad2, gpad, edges, halo,
    xpad, ypad, zpad, vpad, spread, from_x, of_x, from_z, arrived, varp, direc, direc_lo,
    sums, near_sums, total_sums, far_sums,
    own_sem, ens_send, ens_recv, obs_send, obs_recv, group_recv, halo_send, halo_recv,
    x_send, x_recv, z_send, z_recv, rs_send, rs_recv, ag_send, ag_recv, lo_send, lo_recv, sc_send, sc_recv,
):
    me = lax.axis_index("member")
    band = lax.axis_index("band")
    rest = n_member - 1
    cols = lon // LANE
    wide = lat + 2 * HALO
    mid = lat + 2 * HALF
    rows = levels * lat
    up = lax.rem(band + 1, n_band)
    down = lax.rem(band + n_band - 1, n_band)
    my_x, my_z = me // cols, me % cols
    n_x, n_z, n_y = n_member // cols, cols, n_band // 2
    my_y, core = band // 2, band % 2
    my_row = pl.multiple_of(my_x * 8, 8)
    my_col = pl.multiple_of(my_z * LANE, LANE)
    last = levels - 1

    def remote(src, dst, send, recv, to_band, to_member):
        return pltpu.make_async_remote_copy(
            src_ref=src, dst_ref=dst, send_sem=send, recv_sem=recv,
            device_id=(to_band, to_member), device_id_type=pl.DeviceIdType.MESH,
        )

    def drain(ref, sem):
        pltpu.make_async_copy(ref, ref, sem).wait()

    def each(first, stop, start):
        def body(k, carry):
            start(k)
            return carry
        lax.fori_loop(first, stop, body, 0)

    def to_members(start):
        each(1, n_member, lambda k: start(k, lax.rem(me + k, n_member)))

    def near(k):
        index = lax.rem(core * n_z + my_z + k, 2 * n_z)
        return my_y * 2 + index // n_z, my_x * n_z + index % n_z

    def far(k):
        index = lax.rem(my_x * n_y + my_y + k, n_x * n_y)
        return (index % n_y) * 2 + core, (index // n_y) * n_z + my_z

    loads = [
        pltpu.make_async_copy(src, dst, own_sem.at[2 + i])
        for i, (src, dst) in enumerate(
            ((root_hbm, root_ref), (idx_hbm, idx_ref), (val_hbm, val_ref), (err_hbm, err_ref))
        )
    ]
    for load in loads:
        load.start()

    barrier = pltpu.get_barrier_semaphore()

    def greet(to_band, to_member):
        pl.semaphore_signal(
            barrier, inc=1, device_id=(to_band, to_member), device_id_type=pl.DeviceIdType.MESH
        )

    to_members(lambda k, peer: greet(band, peer))
    each(0, n_z, lambda k: greet(my_y * 2 + 1 - core, my_x * n_z + k))

    def greet_plane(k):
        greet(lax.rem(my_y + 1 + k // n_x, n_y) * 2 + core, (k % n_x) * n_z + my_z)

    greeted = n_x * (n_y - 1)
    each(0, greeted, greet_plane)
    greet(lax.rem(band + n_band + 2 * core - 1, n_band), me)
    greeted += n_member - 1 + n_z + 1

    own = pltpu.make_async_copy(ens_ref, ext.at[:, :, pl.ds(HALO, lat), :], own_sem.at[0])
    own.start()
    own_var = pltpu.make_async_copy(
        var_ref.at[:, pl.ds(my_row, 8), pl.ds(my_col, LANE)], varp, own_sem.at[1]
    )
    own_var.start()

    for load in loads:
        load.wait()

    flags = [(root_ref[it] == me).astype(F32) for it in range(ITERS)]
    for j in range(n_member):
        at = pl.ds(j * LANE, LANE)
        parts = [idx_ref[0:1, at].astype(F32), val_ref[0:1, at], err_ref[0:1, at]]
        lines = [part * flags[it] for it in range(ITERS) for part in parts]
        send_obs[j] = jnp.concatenate(lines + [jnp.zeros((2, LANE), F32)], axis=0)

    pl.semaphore_wait(barrier, greeted)

    to_members(
        lambda k, peer: remote(
            send_obs.at[peer], got_obs.at[k - 1], obs_send.at[0], obs_recv.at[0], band, peer
        ).start()
    )
    ens_up = remote(
        ens_ref.at[:, :, pl.ds(lat - HALO, HALO), :], ext.at[:, :, pl.ds(0, HALO), :],
        ens_send.at[0], ens_recv.at[0], up, me,
    )
    ens_down = remote(
        ens_ref.at[:, :, pl.ds(0, HALO), :], ext.at[:, :, pl.ds(HALO + lat, HALO), :],
        ens_send.at[1], ens_recv.at[1], down, me,
    )
    ens_up.start()
    ens_down.start()

    shape = (2 * BLK, BLK)
    wlon[...] = taps(iota(shape, 1) - iota(shape, 0) + LANE, iota(shape, 0) >= 0)
    shape = (QUAD * mid, QUAD * wide)
    target, source = iota(shape, 0), iota(shape, 1)
    row_out = band * lat - HALF + target % mid
    row_in = band * lat - HALO + source % wide
    all_rows = n_band * lat
    lat1[...] = taps(
        row_in - row_out,
        (target // mid == source // wide)
        & (row_out >= 0) & (row_out < all_rows) & (row_in >= 0) & (row_in < all_rows),
    )
    shape = (QUAD * lat, QUAD * mid)
    target, source = iota(shape, 0), iota(shape, 1)
    lat2[...] = taps(source % mid - HALF - target % lat, target // lat == source // mid)

    drain(got_obs, obs_recv.at[0])
    obs[me] = send_obs[me] + jnp.sum(got_obs[...], axis=0)
    to_members(
        lambda k, peer: remote(
            obs.at[me], obs.at[me], obs_send.at[1], group_recv.at[me // GROUP], band, peer
        ).start()
    )

    groups = n_member // GROUP
    width = GROUP * LANE

    def line(g, which):
        return jnp.concatenate([obs[g * GROUP + j, which : which + 1, :] for j in range(GROUP)], axis=1)

    def columns(g):
        return pl.ds(pl.multiple_of(g * width, width), width)

    def each_group(step):
        def body(g, carry):
            step(g)
            return carry
        lax.fori_loop(0, groups, body, 0)

    def hot_of(it, g):
        column = line(g, 3 * it).astype(jnp.int32) % lon
        for r in range(0, lon, LANE):
            hit = iota((LANE, width), 0) + r == column
            hot[r : r + LANE, columns(g)] = jnp.where(hit, 1.0, 0.0).astype(BF16)

    nt = (((1,), (1,)), ((), ()))

    def gather(it):
        field = direc[it - 1].reshape(rows, lon)

        def step(g):
            row = line(g, 3 * it).astype(jnp.int32) // lon
            level, in_level = row // lat, row % lat
            line_of = (in_level // 8) * (8 * levels) + level * 8 + in_level % 8
            found = jnp.dot(field, hot[:, columns(g)], preferred_element_type=F32)
            found = jnp.where(iota((rows, width), 0) == line_of, found, 0.0)
            reached[:, columns(g)] = jnp.sum(found, axis=0, keepdims=True)
        each_group(step)

    def terms_of(it, scale, g):
        values = line(g, 3 * it + 1)
        errors = line(g, 3 * it + 2)
        row = line(g, 3 * it).astype(jnp.int32) // lon
        departure = values
        if it > 0:
            departure = values - scale * reached[:, columns(g)]
        weight = huber_edge / jnp.maximum(jnp.abs(departure / errors), huber_edge)
        square = errors * errors
        hit = iota((rows, width), 0) == row
        for i, part in enumerate(split(weight * departure / square)):
            lhs[i * rows : (i + 1) * rows, columns(g)] = jnp.where(hit, part, 0.0).astype(BF16)
        mine = iota((8 * levels, width), 0)
        hit = (mine // 8) * lat + my_row + mine % 8 == row
        for i, part in enumerate(split(weight / square)):
            a = i * 8 * levels
            lhs2[a : a + 8 * levels, columns(g)] = jnp.where(hit, part, 0.0).astype(BF16)

    def halos(it, b):
        at = pl.ds(b * BLK, BLK)
        return [
            remote(
                edges.at[it, :, pl.ds((1 - side) * (lat - HALO), HALO), at], halo.at[it, side, :, :, at],
                halo_send.at[it, side, b], halo_recv.at[it, side, b], to, me,
            )
            for side, to in enumerate((up, down))
        ]

    def scatter(it):
        for b in range(lon // BLK):
            at = slice(b * BLK, (b + 1) * BLK)
            both = lax.dot_general(lhs[...], hot[at, :], nt, preferred_element_type=F32)
            block = both[:rows] + both[rows:]
            edges[it, :, :, at] = block.reshape(levels, lat, BLK).astype(BF16)
            gpad[it, :, :, at] = block.reshape(levels, lat, BLK)
            for copy in halos(it, b):
                copy.start()
        grad2[...] = lax.dot_general(
            lhs2[...], hot[pl.ds(my_col, LANE), :], nt, preferred_element_type=F32
        )

    def lon_filter(padded, store):
        for c in range(0, lon, BLK):
            at = slice(c, c + BLK)
            store(at, jnp.dot(padded[:, c : c + 2 * BLK], wlon[...], preferred_element_type=F32).astype(BF16))

    def put_padded(ref, at, block):
        ref[:, LANE + at.start : LANE + at.stop] = block
        if at.start == 0:
            ref[:, LANE + lon :] = block[:, :LANE]
        if at.stop == lon:
            ref[:, :LANE] = block[:, block.shape[1] - LANE :]

    def lon_of_rows(it, level, at_rows, gradients):
        for c in range(0, lon, BLK):
            at = slice(c, c + BLK)
            blocks = []
            for part, gradient in zip(at_rows, gradients):
                mixed = ext[:, level, part, at].astype(F32) * gradient[:, at].astype(F32)[None]
                blocks.append(mixed.astype(BF16).reshape(members_here * (part.stop - part.start), BLK))
            put_padded(xpad, at, jnp.concatenate(blocks, axis=0))

        def store(at, block):
            a = 0
            for part in at_rows:
                length = part.stop - part.start
                size = members_here * length
                ypad[level, :, part, at] = block[a : a + size].reshape(members_here, length, BLK)
                a += size

        lon_filter(xpad, store)

    def filters(it, level):
        lon_of_rows(
            it, level, (slice(0, HALO), slice(HALO + lat, wide)), (halo.at[it, 0, level], halo.at[it, 1, level])
        )
        for h in range(members_here // QUAD):
            who = slice(h * QUAD, (h + 1) * QUAD)
            zs, vs = zpad.at[h], vpad.at[h]
            for c in range(0, lon, BLK):
                at = slice(c, c + BLK)
                first = ypad[level, who, :, at].reshape(QUAD * wide, BLK)
                put_padded(zs, at, jnp.dot(lat1[...], first, preferred_element_type=F32).astype(BF16))

            def store_v(at, block):
                vs[:, at] = block

            lon_filter(zs, store_v)
            for c in range(0, lon, BLK):
                at = slice(c, c + BLK)
                second = jnp.dot(lat2[...], vs[:, at], preferred_element_type=F32).reshape(QUAD, lat, BLK)
                part = jnp.sum(ext[who, level, HALO : HALO + lat, at].astype(F32) * second, axis=0)
                if h == 0:
                    spread[it, level, :, at] = part
                else:
                    spread[it, level, :, at] += part

    steps = []
    fields = []
    my_group = me // GROUP
    for g, size in ((0, GROUP - 1), (None, GROUP)):
        def arrive(k):
            at = lax.rem(my_group + k, groups)
            drain(got_obs.at[pl.ds(0, size)], group_recv.at[at])
            hot_of(0, at)
            terms_of(0, None, at)

        if g == 0:
            arrive(0)
        else:
            each(1, groups, arrive)
    for it in range(ITERS):
        if it > 0:
            each_group(functools.partial(terms_of, it, steps[-1]))
        scatter(it)
        if it == 0:
            own.wait()
            own_var.wait()

        def middle(level, carry):
            lon_of_rows(it, level, (slice(HALO, HALO + lat),), (gpad.at[it, level],))
            return carry

        lax.fori_loop(0, levels, middle, 0)
        if it == 0:
            ens_up.wait()
            ens_down.wait()
        for b in range(lon // BLK):
            for copy in halos(it, b):
                copy.wait()

        def level_body(level, carry):
            filters(it, level)

            @pl.when(level < last)
            def _():
                def send_x(k):
                    to_x = lax.rem(my_x + k, n_x)
                    row = pl.multiple_of(to_x * 8, 8)
                    remote(
                        spread.at[it, level, pl.ds(row, 8), :], from_x.at[it, level, k - 1],
                        x_send.at[it, level], x_recv.at[it, level], band, to_x * n_z + my_z,
                    ).start()

                each(1, n_x, send_x)

            @pl.when(level == last)
            def _():
                def send(k, peer):
                    row = pl.multiple_of((peer // n_z) * 8, 8)
                    col = pl.multiple_of((peer % n_z) * LANE, LANE)
                    remote(
                        spread.at[it, last, pl.ds(row, 8), pl.ds(col, LANE)], arrived.at[it, k - 1],
                        rs_send.at[it], rs_recv.at[it], band, peer,
                    ).start()

                to_members(send)
            return carry

        lax.fori_loop(0, levels, level_body, 0)

        def pass_on(level):
            drain(from_x.at[it, level], x_recv.at[it, level])
            of_x[it, level] = spread[it, level, pl.ds(my_row, 8), :] + jnp.sum(from_x[it, level], axis=0)

            def send_z(k):
                to_z = lax.rem(my_z + k, n_z)
                col = pl.multiple_of(to_z * LANE, LANE)
                remote(
                    of_x.at[it, level, :, pl.ds(col, LANE)], from_z.at[it, level, k - 1],
                    z_send.at[it, level], z_recv.at[it, level], band, my_x * n_z + to_z,
                ).start()

            each(1, n_z, send_z)

        each(0, last, pass_on)

        along = jnp.zeros((8, LANE), F32)
        back = jnp.zeros((8, LANE), F32)
        curve = jnp.zeros((8, LANE), F32)
        pieces = []
        for level in range(levels):
            if level < last:
                drain(from_z.at[it, level], z_recv.at[it, level])
                summed = of_x[it, level, :, pl.ds(my_col, LANE)] + jnp.sum(from_z[it, level], axis=0)
            else:
                drain(arrived.at[it], rs_recv.at[it])
                summed = spread[it, level, pl.ds(my_row, 8), pl.ds(my_col, LANE)] + jnp.sum(arrived[it], axis=0)
            g = gpad[it, level, pl.ds(my_row, 8), pl.ds(my_col, LANE)]
            d = ensemble_share * summed / (members_here * n_member - 1) + static_share * varp[level] * g
            pieces.append(d)
        hi, lo = split(jnp.concatenate(pieces, axis=0))
        direc[it, my_x, :, pl.ds(my_col, LANE)] = hi.astype(BF16)

        def send_piece(k, peer):
            piece = direc.at[it, my_x, :, pl.ds(my_col, LANE)]
            remote(piece, piece, ag_send.at[it], ag_recv.at[it], band, peer).start()

        if it == 0:
            to_members(send_piece)
        for level, d in enumerate(pieces):
            g = gpad[it, level, pl.ds(my_row, 8), pl.ds(my_col, LANE)]
            a = level * 8
            c = grad2[a : a + 8, :] + grad2[a + 8 * levels : a + 8 * levels + 8, :]
            along += g * d
            curve += c * d * d
            if it > 0:
                back += fields[-1][level] * g
        sums[it] = jnp.concatenate(
            [jnp.sum(x, axis=0, keepdims=True) for x in (along, back, curve)] + [jnp.zeros((5, LANE), F32)], axis=0
        )

        def send_sums(k):
            remote(sums.at[it], near_sums.at[it, k - 1], sc_send.at[it, 0], sc_recv.at[it, 0], *near(k)).start()

        each(1, 2 * n_z, send_sums)
        if it > 0:
            to_members(send_piece)
        if it + 1 < ITERS:
            each_group(functools.partial(hot_of, it + 1))
        drain(near_sums.at[it], sc_recv.at[it, 0])
        total_sums[it] = sums[it] + jnp.sum(near_sums[it], axis=0)

        def send_total(k):
            remote(total_sums.at[it], far_sums.at[it, k - 1], sc_send.at[it, 1], sc_recv.at[it, 1], *far(k)).start()

        each(1, n_x * n_y, send_total)
        drain(arrived, ag_recv.at[it])
        if it + 1 < ITERS:
            gather(it + 1)
        drain(far_sums.at[it], sc_recv.at[it, 1])
        total = jnp.sum(total_sums[it] + jnp.sum(far_sums[it], axis=0), axis=1, keepdims=True)
        step = (total[0:1] - total[1:2]) / (total[0:1] + total[2:3])
        steps.append(step)
        fields.append([step * d for d in pieces])
        if it + 1 < ITERS:
            direc_lo[my_x, :, pl.ds(my_col, LANE)] = lo.astype(BF16)

            def send_lo(k, peer):
                piece = direc_lo.at[my_x, :, pl.ds(my_col, LANE)]
                remote(piece, piece, lo_send, lo_recv, band, peer).start()

            to_members(send_lo)

    drain(arrived, lo_recv)
    for r in range(lat // 8):
        first = direc[0, r].astype(F32) + direc_lo[r].astype(F32)
        moved = steps[0] * first + steps[1] * direc[1, r].astype(F32)
        for level in range(levels):
            out_ref[level, r * 8 : r * 8 + 8, :] = moved[level * 8 : level * 8 + 8]

    drain(got_obs, obs_send.at[0])
    drain(got_obs, obs_send.at[1])
    for it in range(ITERS):
        for level in range(last):
            drain(from_x.at[it, level], x_send.at[it, level])
            drain(from_z.at[it, level], z_send.at[it, level])
        drain(arrived.at[it], rs_send.at[it])
        drain(arrived, ag_send.at[it])
        drain(near_sums.at[it], sc_send.at[it, 0])
        drain(far_sums.at[it], sc_send.at[it, 1])
    drain(arrived, lo_send)


def local(n_band, n_member, ensemble, variance, obs_index, obs_value, obs_error, root_ranks):
    members_here, levels, lat, lon = ensemble.shape
    wide, mid, rows = lat + 2 * HALO, lat + 2 * HALF, levels * lat
    halves = members_here // QUAD
    rest = n_member - 1
    dma = pltpu.SemaphoreType.DMA
    vmem = pl.BlockSpec(memory_space=pltpu.VMEM)
    hbm = pl.BlockSpec(memory_space=pltpu.HBM)
    return pl.pallas_call(
        functools.partial(kernel, n_band, n_member, members_here, levels, lat, lon),
        out_shape=jax.ShapeDtypeStruct((levels, lat, lon), F32),
        in_specs=[hbm] * 6,
        out_specs=vmem,
        scratch_shapes=[
            pltpu.SMEM((ITERS,), jnp.int32),
            pltpu.VMEM((1, n_member * LANE), jnp.int32),
            pltpu.VMEM((1, n_member * LANE), F32),
            pltpu.VMEM((1, n_member * LANE), F32),
            pltpu.VMEM((members_here, levels, wide, lon), BF16),
            pltpu.VMEM((2 * BLK, BLK), BF16),
            pltpu.VMEM((QUAD * mid, QUAD * wide), BF16),
            pltpu.VMEM((QUAD * lat, QUAD * mid), BF16),
            pltpu.VMEM((n_member, 8, LANE), F32),
            pltpu.VMEM((rest, 8, LANE), F32),
            pltpu.VMEM((n_member, 8, LANE), F32),
            pltpu.VMEM((lon, n_member * LANE), BF16),
            pltpu.VMEM((2 * rows, n_member * LANE), BF16),
            pltpu.VMEM((2 * 8 * levels, n_member * LANE), BF16),
            pltpu.VMEM((1, n_member * LANE), F32),
            pltpu.VMEM((2 * 8 * levels, LANE), F32),
            pltpu.VMEM((ITERS, levels, lat, lon), F32),
            pltpu.VMEM((ITERS, levels, lat, lon), BF16),
            pltpu.VMEM((ITERS, 2, levels, HALO, lon), BF16),
            pltpu.VMEM((members_here * lat, lon + 2 * LANE), BF16),
            pltpu.VMEM((levels, members_here, wide, lon), BF16),
            pltpu.VMEM((halves, QUAD * mid, lon + 2 * LANE), BF16),
            pltpu.VMEM((halves, QUAD * mid, lon), BF16),
            pltpu.VMEM((ITERS, levels, lat, lon), F32),
            pltpu.VMEM((ITERS, levels - 1, lat // 8 - 1, 8, lon), F32),
            pltpu.VMEM((ITERS, levels - 1, 8, lon), F32),
            pltpu.VMEM((ITERS, levels - 1, lon // LANE - 1, 8, LANE), F32),
            pltpu.VMEM((ITERS, rest, 8, LANE), F32),
            pltpu.VMEM((levels, 8, LANE), F32),
            pltpu.VMEM((ITERS, lat // 8, 8 * levels, lon), BF16),
            pltpu.VMEM((lat // 8, 8 * levels, lon), BF16),
            pltpu.VMEM((ITERS, 8, LANE), F32),
            pltpu.VMEM((ITERS, 2 * (lon // LANE) - 1, 8, LANE), F32),
            pltpu.VMEM((ITERS, 8, LANE), F32),
            pltpu.VMEM((ITERS, (lat // 8) * (n_band // 2) - 1, 8, LANE), F32),
            dma((6,)),
            dma((2,)), dma((2,)),
            dma((2,)), dma((1,)), dma((n_member // GROUP,)),
            dma((ITERS, 2, lon // BLK)), dma((ITERS, 2, lon // BLK)),
            dma((ITERS, levels - 1)), dma((ITERS, levels - 1)),
            dma((ITERS, levels - 1)), dma((ITERS, levels - 1)),
            dma((ITERS,)), dma((ITERS,)),
            dma((ITERS,)), dma((ITERS,)),
            dma, dma,
            dma((ITERS, 2)), dma((ITERS, 2)),
        ],
        compiler_params=pltpu.CompilerParams(
            collective_id=0, has_side_effects=True, vmem_limit_bytes=65500 * 1024
        ),
    )(root_ranks, ensemble, variance, obs_index, obs_value, obs_error)


def solution(mesh):
    in_specs = (
        P("member", None, "band", None),
        P(None, "band", None),
        P("member", "band"),
        P("member", "band"),
        P("member", "band"),
        P(),
    )
    body = functools.partial(local, mesh.shape["band"], mesh.shape["member"])
    return jax.shard_map(body, mesh=mesh, in_specs=in_specs, out_specs=P(None, "band", None), check_vma=False)
```
